32 devices in a mesh: band: 4 (over z), facet: 8 (over y, x, core).
Axes of the slice: x: 2, y: 2, z: 4, core: 2. Of those that a mesh axis runs over, the one named last changes fastest.
Arguments:
- facets: bfloat16 [4, 8, 2, 128, 4096], P('band', 'facet'), may hold values from -6 to 6
- col_window: float32 [4096], replicated, may hold values from 0.25 to 1
- slot_of_subgrid: int32 [12], replicated, may hold values from 0 to 15, as said below
- block_slot: int32 [4, 8, 4], P('band', 'facet'), may hold values from 0 to 1
- block_band: int32 [4, 8, 4], P('band', 'facet'), may hold values from 0 to 2
- block_offset: int32 [4, 8, 4], P('band', 'facet'), may hold values from 0 to 128
- block_weight: float32 [4, 8, 4], P('band', 'facet'), may hold values from 0 to 1
- vis_pos: float32 [4, 8, 4, 2, 2048], P('band', 'facet'), may hold values from 0 to 1
Outputs:
- subgrids: bfloat16 [4, 16, 2, 16, 256], P('band', 'facet')
- visibilities: float32 [4, 8, 4, 2, 2048], P('band', 'facet')
The draws below stay inside these ranges and needn't reach their ends.
Inputs may be any that keep to these rules, and one draw needn't show every extreme that they name: `slot_of_subgrid`: values are distinct; at most 2 subgrids share an owner, and some owner holds 2.
All inputs are finite; a program needn't handle non-finite values.
Results may differ from the reference program's by a relative error of at most 0.009.
Values may be sent and summed in bfloat16 or wider, within the bound.
No kernel may reach another device: no remote copies, remote signals or barrier semaphores. Data moves between devices by JAX's collectives and lax.ppermute only.
A program may use at most 64 MiB of HBM per device.

```python
import math
import jax
import jax.numpy as jnp
from jax import lax

SR = 128
SL = 4096
SG = 256
CR = 16
CAP = 2
VB = 4
NV = 2048
PC = 128
NS = 12
N_BAND = 4
N_FACET = 8


def draw_slot_of_subgrid(key, part):
    first_key = jax.random.fold_in(key, 11)
    second_key = jax.random.fold_in(key, 23)
    total = N_FACET * CAP
    shuffled = jax.random.permutation(first_key, total).astype(jnp.int32)
    full_owner = shuffled[0] // CAP
    ranking = jnp.where(shuffled // CAP == full_owner, 0, 1).astype(jnp.int32)
    order = jnp.argsort(ranking, stable=True)
    chosen = shuffled[order][:NS]
    placing = jax.random.permutation(second_key, NS)
    return jnp.zeros((NS,), jnp.int32).at[placing].set(chosen).astype(jnp.int32)


def place_ends(entries, own_key, smallest, top_value):
    extent = entries.shape
    place = [jax.random.randint(jax.random.fold_in(own_key, axis), (), 0, extent[axis]) for axis in range(len(extent))]
    entries = entries.at[tuple(place)].set(smallest)
    longest = extent.index(max(extent))
    place[longest] = (place[longest] + 1) % extent[longest]
    return entries.at[tuple(place)].set(top_value)


def levels(rng, dims, cuts, smallest, largest):
    level, own = 1.0, jax.random.fold_in(rng, 6)
    for axis_at, parts in cuts:
        steps = jnp.exp(jax.random.uniform(jax.random.fold_in(own, axis_at), (parts,), jnp.float32, smallest / len(cuts), largest / len(cuts)))
        level = level * jnp.repeat(steps, dims[axis_at] // parts).reshape([-1 if axis == axis_at else 1 for axis in range(len(dims))])
    return level


def noise(stream_key, extent, deviation, reach, cuts=(), kind=jnp.bfloat16):
    entries = deviation * jax.random.normal(stream_key, extent, jnp.float32)
    if cuts:
        entries = entries * levels(stream_key, extent, cuts, -0.22, 0.18)
    return jnp.clip(entries, -reach, reach).astype(kind)


def setup_inputs(seed: int = 0) -> dict:
    keys = jax.random.split(jax.random.key(seed), 9)
    facets = noise(keys[0], (N_BAND, N_FACET, 2, SR, SL), 1.0, 6.0, ((0, 4), (1, 8)))
    col_window = jnp.clip(jax.random.uniform(keys[1], (SL,), jnp.float32, 0.25, 1.0), 0.25, 1.0)
    slot_of_subgrid = draw_slot_of_subgrid(jax.random.fold_in(keys[8], 71), 0)
    block_slot = place_ends(jax.random.randint(keys[3], (N_BAND, N_FACET, VB), 0, CAP), jax.random.fold_in(keys[3], 1), 0, CAP - 1).astype(jnp.int32)
    block_band = place_ends(jax.random.randint(keys[4], (N_BAND, N_FACET, VB), 0, N_BAND - 1), jax.random.fold_in(keys[4], 1), 0, (N_BAND - 1) - 1).astype(jnp.int32)
    block_offset = place_ends(jax.random.randint(keys[5], (N_BAND, N_FACET, VB), 0, SG - PC + 1), jax.random.fold_in(keys[5], 1), 0, SG - PC).astype(jnp.int32)
    block_weight = jnp.clip(1.0 * jax.random.uniform(keys[6], (N_BAND, N_FACET, VB), jnp.float32) ** levels(keys[6], (N_BAND, N_FACET, VB), ((0, 4), (1, 8)), -0.2, 0.2), 0.0, 1.0)
    vis_pos = jnp.clip(1.0 * jax.random.uniform(keys[7], (N_BAND, N_FACET, VB, 2, NV), jnp.float32) ** levels(keys[7], (N_BAND, N_FACET, VB, 2, NV), ((0, 4), (1, 8)), -0.2, 0.2), 0.0, 1.0)
    return {"facets": facets, "col_window": col_window, "slot_of_subgrid": slot_of_subgrid, "block_slot": block_slot, "block_band": block_band, "block_offset": block_offset, "block_weight": block_weight, "vis_pos": vis_pos}


kernel_sigma = 1.5
highest = lax.Precision.HIGHEST

def column_table(length, width):
    rows = jnp.arange(length, dtype=jnp.int32)[:, None]
    cols = jnp.arange(width, dtype=jnp.int32)[None, :]
    angle = 2.0 * math.pi / length * (rows * cols % length).astype(jnp.float32)
    return jnp.concatenate([jnp.cos(angle), -jnp.sin(angle)], axis=1).astype(jnp.bfloat16)

def combine(product, height, width):
    real_part = product[..., :height, :width] - product[..., height:, width:]
    imag_part = product[..., :height, width:] + product[..., height:, :width]
    return jnp.stack([real_part, imag_part], axis=-3)

def sky_phases(freqs, cells, total):
    angle = 2.0 * math.pi / total * (freqs[..., None] * cells % total).astype(jnp.float32)
    return jnp.concatenate([jnp.cos(angle), -jnp.sin(angle)], axis=-2).astype(jnp.bfloat16)

def inverse_columns(sigma):
    width = sigma.shape[-1]
    index = jnp.arange(width, dtype=jnp.int32)
    angle = 2.0 * math.pi / width * (index[:, None] * index[None, :] % width).astype(jnp.float32)
    cos_part = jnp.cos(angle) / math.sqrt(width)
    sin_part = jnp.sin(angle) / math.sqrt(width)
    real_in = sigma[..., 0, :, :]
    imag_in = sigma[..., 1, :, :]
    real_part = jnp.matmul(real_in, cos_part, precision=highest) - jnp.matmul(imag_in, sin_part, precision=highest)
    imag_part = jnp.matmul(real_in, sin_part, precision=highest) + jnp.matmul(imag_in, cos_part, precision=highest)
    return jnp.stack([real_part, imag_part], axis=-3).astype(jnp.bfloat16)

def degrid_block(patch, position):
    row_grid = jnp.arange(patch.shape[1], dtype=jnp.float32)[:, None]
    col_grid = jnp.arange(patch.shape[2], dtype=jnp.float32)[:, None]
    row_diff = row_grid - position[0][None, :] * (patch.shape[1] - 1)
    col_diff = col_grid - position[1][None, :] * (patch.shape[2] - 1)
    row_kernel = jnp.exp(-row_diff * row_diff / (2.0 * kernel_sigma * kernel_sigma))
    col_kernel = jnp.exp(-col_diff * col_diff / (2.0 * kernel_sigma * kernel_sigma))
    partial_sum = jnp.einsum('xrc,rv->xcv', patch, row_kernel, precision=highest)
    return lax.optimization_barrier(jnp.sum(partial_sum * col_kernel[None], axis=1))

def reference(facets, col_window, slot_of_subgrid, block_slot, block_band, block_offset, block_weight, vis_pos):
    band_count = facets.shape[0]
    facet_count = facets.shape[1]
    strip_rows = facets.shape[3]
    strip_length = facets.shape[4]
    subgrid_count = slot_of_subgrid.shape[0]
    sky_rows = facet_count * strip_rows
    table = column_table(strip_length, SG).astype(jnp.float32)
    all_cells = jnp.arange(sky_rows, dtype=jnp.int32)

    def facet_spectrum(one_facet):
        windowed = (one_facet.astype(jnp.float32) * col_window).astype(jnp.bfloat16)
        flat = windowed.reshape(2 * strip_rows, strip_length).astype(jnp.float32)
        product = jnp.dot(flat, table, precision=highest)
        return (combine(product, strip_rows, SG) * (1.0 / math.sqrt(strip_length))).astype(jnp.bfloat16)

    def band_subgrids(band_facets):
        spectra = lax.map(facet_spectrum, band_facets)
        spectrum_cat = jnp.concatenate([spectra[:, 0], spectra[:, 1]], axis=-1).astype(jnp.float32)

        def one_subgrid(index):
            freqs = index * CR + jnp.arange(CR, dtype=jnp.int32)
            phases = sky_phases(freqs, all_cells, sky_rows).astype(jnp.float32)
            phases = phases.reshape(2 * CR, facet_count, strip_rows)
            product = jnp.einsum('kfj,fjd->fkd', phases, spectrum_cat, precision=highest)
            terms = (combine(product, CR, SG) * (1.0 / math.sqrt(sky_rows))).astype(jnp.bfloat16)
            sigma = lax.optimization_barrier(jnp.sum(terms.astype(jnp.float32), axis=0))
            return inverse_columns(sigma)
        made = lax.map(one_subgrid, jnp.arange(subgrid_count, dtype=jnp.int32))
        empty = jnp.zeros((facet_count * CAP, 2, CR, SG), jnp.bfloat16)
        return empty.at[slot_of_subgrid].set(made)
    subgrids = lax.map(band_subgrids, facets)
    slot_flat = block_slot.reshape(-1)
    band_flat = block_band.reshape(-1)
    offset_flat = block_offset.reshape(-1)
    weight_flat = block_weight.reshape(-1)
    pos_flat = vis_pos.reshape(-1, 2, vis_pos.shape[-1])
    zero = jnp.zeros((), jnp.int32)

    def one_block(index):
        facet_of = (index // VB % facet_count).astype(jnp.int32)
        lower_band = band_flat[index].astype(jnp.int32)
        slot = (facet_of * CAP + slot_flat[index]).astype(jnp.int32)
        start = offset_flat[index].astype(jnp.int32)
        lower = lax.dynamic_slice(subgrids, (lower_band, slot, zero, zero, start), (1, 1, 2, CR, PC))[0, 0]
        upper = lax.dynamic_slice(subgrids, (lower_band + 1, slot, zero, zero, start), (1, 1, 2, CR, PC))[0, 0]
        weight = weight_flat[index]
        patch = (1.0 - weight) * lower.astype(jnp.float32) + weight * upper.astype(jnp.float32)
        return degrid_block(patch, pos_flat[index])
    visible = lax.map(one_block, jnp.arange(band_count * facet_count * VB, dtype=jnp.int32))
    return (subgrids, visible.reshape(vis_pos.shape))
```

```python
import functools
import math

import jax
import jax.numpy as jnp
import numpy as np
from jax import lax
from jax.experimental import pallas as pl
from jax.experimental.pallas import tpu as pltpu
from jax.sharding import PartitionSpec as P

SG = 256
CR = 16
CAP = 2
PC = 128
HALF = SG // 2

kernel_sigma = 1.5
VMEM = pl.BlockSpec(memory_space=pltpu.VMEM)
SMEM = pl.BlockSpec(memory_space=pltpu.SMEM)
ANY = pl.BlockSpec(memory_space=pl.ANY)


def send_to(k, i, n):
    return i ^ k if n & (n - 1) == 0 else (i + k) % n


def recv_from(k, i, n):
    return i ^ k if n & (n - 1) == 0 else (i - k + n) % n


def column_map(length, width):
    j = np.arange(length // 2)[:, None]
    out = []
    for parity in (0, 1):
        freq = np.arange(parity, width, 2)[None, :]
        forward = np.exp(-2j * np.pi / length * (j * freq % length)) / math.sqrt(length)
        k = np.arange(width // 2)[None, :]
        inverse = np.exp(2j * np.pi / width * (freq.T * k % width)) / math.sqrt(width)
        both = forward @ inverse
        out += [both.real, both.imag]
    return np.concatenate(out, axis=1).astype(jnp.bfloat16)


def front_kernel(
    total, chunks, slot_ref, facets_ref, window_ref, table_ref, spec_ref, phase_ref,
    strip, table, strip_sems, table_sems, subgrid_of
):
    rows, length = strip.shape
    half = length // 2
    width = half // chunks
    strip_rows = rows // 2
    copies = []
    for i in range(chunks):
        cols = pl.ds(i * width, width)
        upper = pl.ds(half + i * width, width)
        copies.append((
            pltpu.make_async_copy(facets_ref.at[:, cols], strip.at[:, cols], strip_sems.at[2 * i]),
            pltpu.make_async_copy(facets_ref.at[:, upper], strip.at[:, upper], strip_sems.at[2 * i + 1]),
            pltpu.make_async_copy(table_ref.at[cols], table.at[cols], table_sems.at[i]),
        ))
    for group in copies:
        for copy in group:
            copy.start()

    facet_count = lax.axis_size("facet")
    chips = facet_count // 2
    facet = lax.axis_index("facet")
    chip = facet // 2
    core = facet % 2
    slots = facet_count * CAP
    for s in range(slots):
        subgrid_of[s] = -1
    for s in range(slot_ref.shape[0]):
        subgrid_of[slot_ref[s]] = s
    step = 2.0 * math.pi / total
    lane = lax.broadcasted_iota(jnp.int32, (CR, strip_rows), 1)
    row = lax.broadcasted_iota(jnp.int32, (CR, strip_rows), 0)
    for side in range(2):
        side_facet = facet if side == 0 else facet ^ 1
        cell = side_facet * strip_rows + lane
        angle = step * lax.rem(row * cell, total).astype(jnp.float32)
        row_cos, row_sin = jnp.cos(angle), jnp.sin(angle)
        first = 2 * side * strip_rows
        left = pl.ds(first, strip_rows)
        right = pl.ds(first + strip_rows, strip_rows)
        for k in range(chips):
            owner = 2 * send_to(k, chip, chips) + core
            for c in range(CAP):
                sub = subgrid_of[owner * CAP + c]
                live = jnp.where(sub >= 0, 1.0, 0.0).astype(jnp.float32)
                base = jnp.maximum(sub, 0) * CR
                turn = step * lax.rem(base * cell[:8], total).astype(jnp.float32)
                base_cos = jnp.cos(turn) * live
                base_sin = jnp.sin(turn) * live
                base_cos = jnp.concatenate([base_cos, base_cos], axis=0)
                base_sin = jnp.concatenate([base_sin, base_sin], axis=0)
                cos = (base_cos * row_cos - base_sin * row_sin).astype(jnp.bfloat16)
                sin = (base_sin * row_cos + base_cos * row_sin).astype(jnp.bfloat16)
                at = (k * CAP + c) * 2 * CR
                phase_ref[pl.ds(at, CR), left] = cos
                phase_ref[pl.ds(at, CR), right] = sin
                phase_ref[pl.ds(at + CR, CR), left] = -sin
                phase_ref[pl.ds(at + CR, CR), right] = cos

    even = odd = None
    for i in range(chunks):
        for copy in copies[i]:
            copy.wait()
        cols = pl.ds(i * width, width)
        upper = pl.ds(half + i * width, width)
        near = strip[:, cols].astype(jnp.float32) * window_ref[:, cols]
        far = strip[:, upper].astype(jnp.float32) * window_ref[:, upper]
        even_part = jnp.dot(
            (near + far).astype(jnp.bfloat16), table[cols, :SG], preferred_element_type=jnp.float32
        )
        odd_part = jnp.dot(
            (near - far).astype(jnp.bfloat16), table[cols, SG:], preferred_element_type=jnp.float32
        )
        even = even_part if even is None else even + even_part
        odd = odd_part if odd is None else odd + odd_part
    n = strip_rows
    even_real = even[:n, :HALF] - even[n:, HALF:]
    even_imag = even[:n, HALF:] + even[n:, :HALF]
    odd_real = odd[:n, :HALF] - odd[n:, HALF:]
    odd_imag = odd[:n, HALF:] + odd[n:, :HALF]
    spec_ref[:n, :HALF] = (even_real + odd_real).astype(jnp.bfloat16)
    spec_ref[:n, HALF:] = (even_real - odd_real).astype(jnp.bfloat16)
    spec_ref[n:, :HALF] = (even_imag + odd_imag).astype(jnp.bfloat16)
    spec_ref[n:, HALF:] = (even_imag - odd_imag).astype(jnp.bfloat16)


def term_kernel(scale, phase_ref, own_ref, other_ref, *out_refs):
    depth = own_ref.shape[0]
    terms = jnp.dot(phase_ref[:, :depth], own_ref[...], preferred_element_type=jnp.float32)
    terms += jnp.dot(phase_ref[:, depth:], other_ref[...], preferred_element_type=jnp.float32)
    terms = (terms * scale).astype(jnp.bfloat16)
    height = CAP * 2 * CR
    for k, out_ref in enumerate(out_refs):
        out_ref[...] = terms[k * height : (k + 1) * height]


def weights_kernel(pos_ref, col_ref, row_ref):
    blocks, width, points = col_ref.shape
    factor = -1.0 / (2.0 * kernel_sigma * kernel_sigma)
    tile = 512
    for v in range(blocks):
        for t in range(0, points, tile):
            at = pl.ds(t, tile)
            diff = lax.broadcasted_iota(jnp.int32, (CR, tile), 0).astype(jnp.float32) - (
                pos_ref[v, 0:1, at] * (CR - 1.0)
            )
            row_ref[v, :, at] = jnp.exp(diff * diff * factor)
            diff = lax.broadcasted_iota(jnp.int32, (width, tile), 0).astype(jnp.float32) - (
                pos_ref[v, 1:2, at] * (width - 1.0)
            )
            col_ref[v, :, at] = jnp.exp(diff * diff * factor).astype(jnp.bfloat16)


def degrid_kernel(bands, slot_ref, band_ref, offset_ref, weight_ref, col_ref, row_ref, *refs):
    sub_refs, out_ref, every = refs[:bands], refs[bands], refs[bands + 1]
    me = lax.axis_index("band")
    for k in range(bands):
        every[recv_from(k, me, bands)] = sub_refs[k][...].astype(jnp.float32)
    blocks = col_ref.shape[0]
    for v in range(blocks):
        low = band_ref[v]
        at = pl.ds(pl.multiple_of(slot_ref[v] * 2 * CR, 2 * CR), 2 * CR)
        weight = weight_ref[v]
        patch = (1.0 - weight) * every[low, at, :] + weight * every[low + 1, at, :]
        patch = pltpu.roll(patch, lax.rem(SG - offset_ref[v], SG), 1)[:, :PC].astype(jnp.bfloat16)
        partial = jnp.dot(patch, col_ref[v], preferred_element_type=jnp.float32)
        out_ref[v, 0:1, :] = jnp.sum(partial[:CR] * row_ref[v], axis=0, keepdims=True)
        out_ref[v, 1:2, :] = jnp.sum(partial[CR:] * row_ref[v], axis=0, keepdims=True)


def local(
    facets, col_window, slot_of_subgrid, block_slot, block_band, block_offset, block_weight, vis_pos
):
    facet_count = lax.axis_size("facet")
    band_count = lax.axis_size("band")
    chips = facet_count // 2
    strip_rows = facets.shape[3]
    length = facets.shape[4]
    sky_rows = facet_count * strip_rows
    blocks, points = vis_pos.shape[2], vis_pos.shape[4]
    height = CAP * 2 * CR
    chunks = 4

    strip = facets.reshape(2 * strip_rows, length)
    table = jnp.asarray(column_map(length, SG))
    spectrum, phases = pl.pallas_call(
        functools.partial(front_kernel, sky_rows, chunks),
        out_shape=(
            jax.ShapeDtypeStruct((2 * strip_rows, SG), jnp.bfloat16),
            jax.ShapeDtypeStruct((chips * height, 4 * strip_rows), jnp.bfloat16),
        ),
        in_specs=[SMEM, ANY, VMEM, ANY],
        out_specs=(VMEM, VMEM),
        scratch_shapes=[
            pltpu.VMEM((2 * strip_rows, length), jnp.bfloat16),
            pltpu.VMEM((length // 2, 2 * SG), jnp.bfloat16),
            pltpu.SemaphoreType.DMA((2 * chunks,)),
            pltpu.SemaphoreType.DMA((chunks,)),
            pltpu.SMEM((facet_count * CAP,), jnp.int32),
        ],
        compiler_params=pltpu.CompilerParams(vmem_limit_bytes=32 * 2**20),
        name="front",
    )(slot_of_subgrid, strip, col_window.reshape(1, length), table)

    other = lax.ppermute(spectrum, "facet", [(i, i ^ 1) for i in range(facet_count)])
    term_shape = jax.ShapeDtypeStruct((height, SG), jnp.bfloat16)
    terms = pl.pallas_call(
        functools.partial(term_kernel, 1.0 / math.sqrt(sky_rows)),
        out_shape=(term_shape,) * chips,
        in_specs=[VMEM] * 3,
        out_specs=(VMEM,) * chips,
        compiler_params=pltpu.CompilerParams(vmem_limit_bytes=16 * 2**20),
        name="terms",
    )(phases, spectrum, other)
    arrived = [terms[0]] + [
        lax.ppermute(
            terms[k],
            "facet",
            [(i, 2 * send_to(k, i // 2, chips) + i % 2) for i in range(facet_count)],
        )
        for k in range(1, chips)
    ]
    total = arrived[0].astype(jnp.float32)
    for part in arrived[1:]:
        total = total + part.astype(jnp.float32)
    owned = total.astype(jnp.bfloat16)

    col_kernel, row_kernel = pl.pallas_call(
        weights_kernel,
        out_shape=(
            jax.ShapeDtypeStruct((blocks, PC, points), jnp.bfloat16),
            jax.ShapeDtypeStruct((blocks, CR, points), jnp.float32),
        ),
        in_specs=[VMEM],
        out_specs=(VMEM, VMEM),
        compiler_params=pltpu.CompilerParams(vmem_limit_bytes=16 * 2**20),
        cost_estimate=pl.CostEstimate(flops=8 * blocks * PC * points, bytes_accessed=0, transcendentals=blocks * PC * points),
        name="weights",
    )(vis_pos.reshape(blocks, 2, points))

    subs = [owned] + [
        lax.ppermute(owned, "band", [(i, send_to(k, i, band_count)) for i in range(band_count)])
        for k in range(1, band_count)
    ]
    visible = pl.pallas_call(
        functools.partial(degrid_kernel, band_count),
        out_shape=jax.ShapeDtypeStruct((blocks, 2, points), jnp.float32),
        in_specs=[SMEM] * 4 + [VMEM] * (2 + band_count),
        out_specs=VMEM,
        scratch_shapes=[pltpu.VMEM((band_count, height, SG), jnp.float32)],
        compiler_params=pltpu.CompilerParams(vmem_limit_bytes=24 * 2**20),
        name="degrid",
    )(
        block_slot.reshape(blocks), block_band.reshape(blocks), block_offset.reshape(blocks),
        block_weight.reshape(blocks), col_kernel, row_kernel, *subs
    )
    return (
        owned.reshape(1, CAP, 2, CR, SG),
        visible.reshape(1, 1, blocks, 2, points),
    )


def solution(mesh):
    in_specs = (
        P("band", "facet", None, None, None),
        P(),
        P(),
        P("band", "facet", None),
        P("band", "facet", None),
        P("band", "facet", None),
        P("band", "facet", None),
        P("band", "facet", None, None, None),
    )
    out_specs = (P("band", "facet", None, None, None), P("band", "facet", None, None, None))
    return jax.shard_map(local, mesh=mesh, in_specs=in_specs, out_specs=out_specs, check_vma=False)
```

```python
import functools
import math

import jax
import jax.numpy as jnp
import numpy as np
from jax import lax
from jax.experimental import pallas as pl
from jax.experimental.pallas import tpu as pltpu
from jax.sharding import PartitionSpec as P

SG = 256
CR = 16
CAP = 2
PC = 128
HALF = SG // 2

kernel_sigma = 1.5
VMEM = pl.BlockSpec(memory_space=pltpu.VMEM)
SMEM = pl.BlockSpec(memory_space=pltpu.SMEM)
HBM = pl.BlockSpec(memory_space=pltpu.HBM)


def send_to(k, i, n):
    return i ^ k if n & (n - 1) == 0 else (i + k) % n


def recv_from(k, i, n):
    return i ^ k if n & (n - 1) == 0 else (i - k + n) % n


def column_map(length, width):
    j = np.arange(length // 2)[:, None]
    out = []
    for parity in (0, 1):
        freq = np.arange(parity, width, 2)[None, :]
        forward = np.exp(-2j * np.pi / length * (j * freq % length)) / math.sqrt(length)
        k = np.arange(width // 2)[None, :]
        inverse = np.exp(2j * np.pi / width * (freq.T * k % width)) / math.sqrt(width)
        both = forward @ inverse
        out += [both.real, both.imag]
    return np.concatenate(out, axis=1).astype(jnp.bfloat16)


def front_kernel(
    total, chunks, slot_hbm, facets_ref, window_hbm, table_ref, spec_ref, phase_ref,
    strip, table, window_ref, slot_ref, strip_sems, table_sems, small_sems, subgrid_of
):
    rows, length = strip.shape
    half = length // 2
    width = half // chunks
    strip_rows = rows // 2
    slot_copy = pltpu.make_async_copy(slot_hbm, slot_ref, small_sems.at[0])
    window_copy = pltpu.make_async_copy(window_hbm, window_ref, small_sems.at[1])
    slot_copy.start()
    window_copy.start()
    copies = []
    for i in range(chunks):
        cols = pl.ds(i * width, width)
        upper = pl.ds(half + i * width, width)
        copies.append((
            pltpu.make_async_copy(facets_ref.at[:, cols], strip.at[:, cols], strip_sems.at[2 * i]),
            pltpu.make_async_copy(facets_ref.at[:, upper], strip.at[:, upper], strip_sems.at[2 * i + 1]),
            pltpu.make_async_copy(table_ref.at[cols], table.at[cols], table_sems.at[i]),
        ))
    for group in copies:
        for copy in group:
            copy.start()

    facet_count = lax.axis_size("facet")
    chips = facet_count // 2
    facet = lax.axis_index("facet")
    chip = facet // 2
    core = facet % 2
    slots = facet_count * CAP
    for s in range(slots):
        subgrid_of[s] = -1
    slot_copy.wait()
    for s in range(slot_ref.shape[0]):
        subgrid_of[slot_ref[s]] = s
    step = 2.0 * math.pi / total
    lane = lax.broadcasted_iota(jnp.int32, (CR, strip_rows), 1)
    row = lax.broadcasted_iota(jnp.int32, (CR, strip_rows), 0)
    for side in range(2):
        side_facet = facet if side == 0 else facet ^ 1
        cell = side_facet * strip_rows + lane
        angle = step * lax.rem(row * cell, total).astype(jnp.float32)
        row_cos, row_sin = jnp.cos(angle), jnp.sin(angle)
        first = 2 * side * strip_rows
        left = pl.ds(first, strip_rows)
        right = pl.ds(first + strip_rows, strip_rows)
        for k in range(chips):
            owner = 2 * send_to(k, chip, chips) + core
            for c in range(CAP):
                sub = subgrid_of[owner * CAP + c]
                live = jnp.where(sub >= 0, 1.0, 0.0).astype(jnp.float32)
                base = jnp.maximum(sub, 0) * CR
                turn = step * lax.rem(base * cell[:8], total).astype(jnp.float32)
                base_cos = jnp.cos(turn) * live
                base_sin = jnp.sin(turn) * live
                base_cos = jnp.concatenate([base_cos, base_cos], axis=0)
                base_sin = jnp.concatenate([base_sin, base_sin], axis=0)
                cos = (base_cos * row_cos - base_sin * row_sin).astype(jnp.bfloat16)
                sin = (base_sin * row_cos + base_cos * row_sin).astype(jnp.bfloat16)
                at = (k * CAP + c) * 2 * CR
                phase_ref[pl.ds(at, CR), left] = cos
                phase_ref[pl.ds(at, CR), right] = sin
                phase_ref[pl.ds(at + CR, CR), left] = -sin
                phase_ref[pl.ds(at + CR, CR), right] = cos

    window_copy.wait()
    even = odd = None
    for i in range(chunks):
        for copy in copies[i]:
            copy.wait()
        cols = pl.ds(i * width, width)
        upper = pl.ds(half + i * width, width)
        near = strip[:, cols].astype(jnp.float32) * window_ref[:, cols]
        far = strip[:, upper].astype(jnp.float32) * window_ref[:, upper]
        even_part = jnp.dot(
            (near + far).astype(jnp.bfloat16), table[cols, :SG], preferred_element_type=jnp.float32
        )
        odd_part = jnp.dot(
            (near - far).astype(jnp.bfloat16), table[cols, SG:], preferred_element_type=jnp.float32
        )
        even = even_part if even is None else even + even_part
        odd = odd_part if odd is None else odd + odd_part
    n = strip_rows
    even_real = even[:n, :HALF] - even[n:, HALF:]
    even_imag = even[:n, HALF:] + even[n:, :HALF]
    odd_real = odd[:n, :HALF] - odd[n:, HALF:]
    odd_imag = odd[:n, HALF:] + odd[n:, :HALF]
    spec_ref[:n, :HALF] = (even_real + odd_real).astype(jnp.bfloat16)
    spec_ref[:n, HALF:] = (even_real - odd_real).astype(jnp.bfloat16)
    spec_ref[n:, :HALF] = (even_imag + odd_imag).astype(jnp.bfloat16)
    spec_ref[n:, HALF:] = (even_imag - odd_imag).astype(jnp.bfloat16)


def term_kernel(scale, phase_ref, own_ref, other_ref, *out_refs):
    depth = own_ref.shape[0]
    terms = jnp.dot(phase_ref[:, :depth], own_ref[...], preferred_element_type=jnp.float32)
    terms += jnp.dot(phase_ref[:, depth:], other_ref[...], preferred_element_type=jnp.float32)
    terms = (terms * scale).astype(jnp.bfloat16)
    height = CAP * 2 * CR
    for k, out_ref in enumerate(out_refs):
        out_ref[...] = terms[k * height : (k + 1) * height]


def weights_kernel(
    bands, slot_ref, band_ref, offset_ref, weight_ref, pos_ref, col_ref, row_ref, mix_ref, lane_ref
):
    blocks, width, points = col_ref.shape
    factor = -1.0 / (2.0 * kernel_sigma * kernel_sigma)
    tile = 512
    me = lax.axis_index("band")
    column = lax.broadcasted_iota(jnp.int32, (width, tile), 0).astype(jnp.float32)
    row = lax.broadcasted_iota(jnp.int32, (CR, tile), 0).astype(jnp.float32)
    for v in range(blocks):
        low = band_ref[v]
        slot = slot_ref[v]
        weight = weight_ref[v]
        for k in range(bands):
            band = recv_from(k, me, bands)
            share = jnp.where(band == low, 1.0 - weight, jnp.where(band == low + 1, weight, 0.0))
            for c in range(CAP):
                mix_ref[v, k * CAP + c] = jnp.full((8, 128), jnp.where(slot == c, share, 0.0), jnp.float32)
        lane_ref[v] = offset_ref[v] + lax.broadcasted_iota(jnp.int32, (2 * CR, PC), 1)
        for t in range(0, points, tile):
            at = pl.ds(t, tile)
            diff = row - pos_ref[v, 0:1, at] * (CR - 1.0)
            row_ref[v, :, at] = jnp.exp(diff * diff * factor)
            diff = column - pos_ref[v, 1:2, at] * (PC - 1.0)
            col_ref[v, :, at] = jnp.exp(diff * diff * factor).astype(jnp.bfloat16)


def degrid_kernel(bands, mix_ref, lane_ref, col_ref, row_ref, *refs):
    sub_refs, out_ref = refs[:bands], refs[bands]
    height = 2 * CR
    held = [
        sub_refs[k][c * height : (c + 1) * height, :].astype(jnp.float32)
        for k in range(bands)
        for c in range(CAP)
    ]
    for v in range(col_ref.shape[0]):
        halves = []
        for first in (0, HALF):
            mixed = None
            for i, sub in enumerate(held):
                share = jnp.concatenate([mix_ref[v, i]] * (height // 8), axis=0)
                part = sub[:, first : first + HALF] * share
                mixed = part if mixed is None else mixed + part
            halves.append(mixed)
        lane = lane_ref[v]
        within = lax.rem(lane, HALF)
        near, far = (jnp.take_along_axis(half, within, axis=1, mode="promise_in_bounds") for half in halves)
        patch = jnp.where(lane < HALF, near, far)
        partial = jnp.dot(
            patch.astype(jnp.bfloat16), col_ref[v], preferred_element_type=jnp.float32
        )
        out_ref[v, 0:1, :] = jnp.sum(partial[:CR] * row_ref[v], axis=0, keepdims=True)
        out_ref[v, 1:2, :] = jnp.sum(partial[CR:] * row_ref[v], axis=0, keepdims=True)


def local(
    facets, col_window, slot_of_subgrid, block_slot, block_band, block_offset, block_weight, vis_pos
):
    facet_count = lax.axis_size("facet")
    band_count = lax.axis_size("band")
    chips = facet_count // 2
    strip_rows = facets.shape[3]
    length = facets.shape[4]
    sky_rows = facet_count * strip_rows
    blocks, points = vis_pos.shape[2], vis_pos.shape[4]
    height = CAP * 2 * CR
    chunks = 4

    strip = facets.reshape(2 * strip_rows, length)
    table = jnp.asarray(column_map(length, SG))
    spectrum, phases = pl.pallas_call(
        functools.partial(front_kernel, sky_rows, chunks),
        out_shape=(
            jax.ShapeDtypeStruct((2 * strip_rows, SG), jnp.bfloat16),
            jax.ShapeDtypeStruct((chips * height, 4 * strip_rows), jnp.bfloat16),
        ),
        in_specs=[HBM] * 4,
        out_specs=(VMEM, VMEM),
        scratch_shapes=[
            pltpu.VMEM((2 * strip_rows, length), jnp.bfloat16),
            pltpu.VMEM((length // 2, 2 * SG), jnp.bfloat16),
            pltpu.VMEM((1, length), jnp.float32),
            pltpu.SMEM(slot_of_subgrid.shape, jnp.int32),
            pltpu.SemaphoreType.DMA((2 * chunks,)),
            pltpu.SemaphoreType.DMA((chunks,)),
            pltpu.SemaphoreType.DMA((2,)),
            pltpu.SMEM((facet_count * CAP,), jnp.int32),
        ],
        compiler_params=pltpu.CompilerParams(vmem_limit_bytes=32 * 2**20),
        name="front",
    )(*(
        pltpu.with_memory_space_constraint(x, pltpu.HBM)
        for x in (slot_of_subgrid, strip, col_window.reshape(1, length), table)
    ))

    other = lax.ppermute(spectrum, "facet", [(i, i ^ 1) for i in range(facet_count)])
    term_shape = jax.ShapeDtypeStruct((height, SG), jnp.bfloat16)
    terms = pl.pallas_call(
        functools.partial(term_kernel, 1.0 / math.sqrt(sky_rows)),
        out_shape=(term_shape,) * chips,
        in_specs=[VMEM] * 3,
        out_specs=(VMEM,) * chips,
        compiler_params=pltpu.CompilerParams(vmem_limit_bytes=16 * 2**20),
        name="terms",
    )(phases, spectrum, other)
    arrived = [terms[0]] + [
        lax.ppermute(
            terms[k],
            "facet",
            [(i, 2 * send_to(k, i // 2, chips) + i % 2) for i in range(facet_count)],
        )
        for k in range(1, chips)
    ]
    total = arrived[0].astype(jnp.float32)
    for part in arrived[1:]:
        total = total + part.astype(jnp.float32)
    owned = total.astype(jnp.bfloat16)

    col_kernel, row_kernel, mix, lanes = pl.pallas_call(
        functools.partial(weights_kernel, band_count),
        out_shape=(
            jax.ShapeDtypeStruct((blocks, PC, points), jnp.bfloat16),
            jax.ShapeDtypeStruct((blocks, CR, points), jnp.float32),
            jax.ShapeDtypeStruct((blocks, band_count * CAP, 8, 128), jnp.float32),
            jax.ShapeDtypeStruct((blocks, 2 * CR, PC), jnp.int32),
        ),
        in_specs=[SMEM] * 4 + [VMEM],
        out_specs=(VMEM,) * 4,
        compiler_params=pltpu.CompilerParams(vmem_limit_bytes=16 * 2**20),
        cost_estimate=pl.CostEstimate(
            flops=8 * blocks * PC * points, bytes_accessed=0, transcendentals=blocks * PC * points
        ),
        name="weights",
    )(
        block_slot.reshape(blocks), block_band.reshape(blocks), block_offset.reshape(blocks),
        block_weight.reshape(blocks), vis_pos.reshape(blocks, 2, points),
    )

    subs = [owned] + [
        lax.ppermute(owned, "band", [(i, send_to(k, i, band_count)) for i in range(band_count)])
        for k in range(1, band_count)
    ]
    visible = pl.pallas_call(
        functools.partial(degrid_kernel, band_count),
        out_shape=jax.ShapeDtypeStruct((blocks, 2, points), jnp.float32),
        in_specs=[VMEM] * (4 + band_count),
        out_specs=VMEM,
        compiler_params=pltpu.CompilerParams(vmem_limit_bytes=24 * 2**20),
        name="degrid",
    )(mix, lanes, col_kernel, row_kernel, *subs)
    return (
        owned.reshape(1, CAP, 2, CR, SG),
        visible.reshape(1, 1, blocks, 2, points),
    )


def solution(mesh):
    in_specs = (
        P("band", "facet", None, None, None),
        P(),
        P(),
        P("band", "facet", None),
        P("band", "facet", None),
        P("band", "facet", None),
        P("band", "facet", None),
        P("band", "facet", None, None, None),
    )
    out_specs = (P("band", "facet", None, None, None), P("band", "facet", None, None, None))
    return jax.shard_map(local, mesh=mesh, in_specs=in_specs, out_specs=out_specs, check_vma=False)
```

```python
import functools
import math

import jax
import jax.numpy as jnp
import numpy as np
from jax import lax
from jax.experimental import pallas as pl
from jax.experimental.pallas import tpu as pltpu
from jax.sharding import PartitionSpec as P

SG = 256
CR = 16
CAP = 2
PC = 128
HALF = SG // 2

kernel_sigma = 1.5
VMEM = pl.BlockSpec(memory_space=pltpu.VMEM)
SMEM = pl.BlockSpec(memory_space=pltpu.SMEM)
HBM = pl.BlockSpec(memory_space=pltpu.HBM)


def send_to(k, i, n):
    return i ^ k if n & (n - 1) == 0 else (i + k) % n


def recv_from(k, i, n):
    return i ^ k if n & (n - 1) == 0 else (i - k + n) % n


def column_map(length, width):
    j = np.arange(length // 2)[:, None]
    out = []
    for parity in (0, 1):
        freq = np.arange(parity, width, 2)[None, :]
        forward = np.exp(-2j * np.pi / length * (j * freq % length)) / math.sqrt(length)
        k = np.arange(width // 2)[None, :]
        inverse = np.exp(2j * np.pi / width * (freq.T * k % width)) / math.sqrt(width)
        both = forward @ inverse
        out += [both.real, both.imag]
    return np.concatenate(out, axis=1).astype(jnp.bfloat16)


def front_kernel(
    total, chunks, slot_hbm, facets_ref, window_hbm, table_ref, spec_ref, phase_ref,
    strip, table, window_ref, slot_ref, strip_sems, table_sems, small_sems, subgrid_of
):
    rows, length = strip.shape
    half = length // 2
    width = half // chunks
    strip_rows = rows // 2
    slot_copy = pltpu.make_async_copy(slot_hbm, slot_ref, small_sems.at[0])
    window_copy = pltpu.make_async_copy(window_hbm, window_ref, small_sems.at[1])
    slot_copy.start()
    window_copy.start()
    copies = []
    for i in range(chunks):
        cols = pl.ds(i * width, width)
        upper = pl.ds(half + i * width, width)
        copies.append((
            pltpu.make_async_copy(facets_ref.at[:, cols], strip.at[:, cols], strip_sems.at[2 * i]),
            pltpu.make_async_copy(facets_ref.at[:, upper], strip.at[:, upper], strip_sems.at[2 * i + 1]),
            pltpu.make_async_copy(table_ref.at[cols], table.at[cols], table_sems.at[i]),
        ))
    for group in copies:
        for copy in group:
            copy.start()

    facet_count = lax.axis_size("facet")
    chips = facet_count // 2
    facet = lax.axis_index("facet")
    chip = facet // 2
    for s in range(facet_count * CAP):
        subgrid_of[s] = -1
    slot_copy.wait()
    for s in range(slot_ref.shape[0]):
        subgrid_of[slot_ref[s]] = s

    step = 2.0 * math.pi / total
    lane = lax.broadcasted_iota(jnp.int32, (CR, strip_rows), 1)
    row = lax.broadcasted_iota(jnp.int32, (CR, strip_rows), 0)
    cells, row_trig = [], []
    for side in range(2):
        cell = (facet if side == 0 else facet ^ 1) * strip_rows + lane
        angle = step * lax.rem(row * cell, total).astype(jnp.float32)
        cells.append(cell)
        row_trig.append((jnp.cos(angle), jnp.sin(angle)))

    def write_phases(ref, first_row, owner_chip, side):
        row_cos, row_sin = row_trig[side]
        left = pl.ds(2 * side * strip_rows, strip_rows)
        right = pl.ds((2 * side + 1) * strip_rows, strip_rows)
        for c in range(2 * CAP):
            sub = subgrid_of[owner_chip * 2 * CAP + c]
            live = jnp.where(sub >= 0, 1.0, 0.0).astype(jnp.float32)
            base = jnp.maximum(sub, 0) * CR
            turn = step * lax.rem(base * cells[side][:8], total).astype(jnp.float32)
            base_cos = jnp.cos(turn) * live
            base_sin = jnp.sin(turn) * live
            base_cos = jnp.concatenate([base_cos, base_cos], axis=0)
            base_sin = jnp.concatenate([base_sin, base_sin], axis=0)
            cos = (base_cos * row_cos - base_sin * row_sin).astype(jnp.bfloat16)
            sin = (base_sin * row_cos + base_cos * row_sin).astype(jnp.bfloat16)
            at = first_row + c * 2 * CR
            ref[pl.ds(at, CR), left] = cos
            ref[pl.ds(at, CR), right] = sin
            ref[pl.ds(at + CR, CR), left] = -sin
            ref[pl.ds(at + CR, CR), right] = cos

    height = 2 * CAP * 2 * CR
    @pl.when(facet % 2 == 0)
    def _():
        for side in range(2):
            write_phases(phase_ref, 0, chip, side)

    @pl.when(facet % 2 == 1)
    def _():
        for side in range(2):
            for k in range(1, chips):
                write_phases(phase_ref, (k - 1) * height, send_to(k, chip, chips), side)

    window_copy.wait()
    even = odd = None
    for i in range(chunks):
        for copy in copies[i]:
            copy.wait()
        cols = pl.ds(i * width, width)
        upper = pl.ds(half + i * width, width)
        near = strip[:, cols].astype(jnp.float32) * window_ref[:, cols]
        far = strip[:, upper].astype(jnp.float32) * window_ref[:, upper]
        even_part = jnp.dot(
            (near + far).astype(jnp.bfloat16), table[cols, :SG], preferred_element_type=jnp.float32
        )
        odd_part = jnp.dot(
            (near - far).astype(jnp.bfloat16), table[cols, SG:], preferred_element_type=jnp.float32
        )
        even = even_part if even is None else even + even_part
        odd = odd_part if odd is None else odd + odd_part
    n = strip_rows
    even_real = even[:n, :HALF] - even[n:, HALF:]
    even_imag = even[:n, HALF:] + even[n:, :HALF]
    odd_real = odd[:n, :HALF] - odd[n:, HALF:]
    odd_imag = odd[:n, HALF:] + odd[n:, :HALF]
    spec_ref[:n, :HALF] = (even_real + odd_real).astype(jnp.bfloat16)
    spec_ref[:n, HALF:] = (even_real - odd_real).astype(jnp.bfloat16)
    spec_ref[n:, :HALF] = (even_imag + odd_imag).astype(jnp.bfloat16)
    spec_ref[n:, HALF:] = (even_imag - odd_imag).astype(jnp.bfloat16)


def term_kernel(scale, phase_ref, own_ref, other_ref, *out_refs):
    depth = own_ref.shape[0]
    height = out_refs[0].shape[0]

    def write_terms(k):
        at = pl.ds(k * height, height)
        terms = jnp.dot(phase_ref[at, :depth], own_ref[...], preferred_element_type=jnp.float32)
        terms += jnp.dot(phase_ref[at, depth:], other_ref[...], preferred_element_type=jnp.float32)
        out_refs[k][...] = (terms * scale).astype(jnp.bfloat16)

    write_terms(0)

    @pl.when(lax.axis_index("facet") % 2 == 1)
    def _():
        for k in range(1, len(out_refs)):
            write_terms(k)


def weights_kernel(
    bands, slot_ref, band_ref, offset_ref, weight_ref, pos_ref, after_ref, col_ref, row_ref, mix_ref, lane_ref, core_ref
):
    blocks, width, points = col_ref.shape
    factor = -1.0 / (2.0 * kernel_sigma * kernel_sigma)
    tile = 512
    me = lax.axis_index("band")
    core_ref[...] = jnp.full(core_ref.shape, lax.axis_index("facet") % 2, jnp.int32)
    column = lax.broadcasted_iota(jnp.int32, (width, tile), 0).astype(jnp.float32)
    row = lax.broadcasted_iota(jnp.int32, (CR, tile), 0).astype(jnp.float32)
    for v in range(blocks):
        low = band_ref[v]
        slot = slot_ref[v]
        weight = weight_ref[v]
        for k in range(bands):
            band = recv_from(k, me, bands)
            share = jnp.where(band == low, 1.0 - weight, jnp.where(band == low + 1, weight, 0.0))
            for c in range(CAP):
                mix_ref[v, k * CAP + c] = jnp.full((8, 128), jnp.where(slot == c, share, 0.0), jnp.float32)
        lane_ref[v] = offset_ref[v] + lax.broadcasted_iota(jnp.int32, (2 * CR, PC), 1)
        for t in range(0, points, tile):
            at = pl.ds(t, tile)
            diff = row - pos_ref[v, 0:1, at] * (CR - 1.0)
            row_ref[v, :, at] = jnp.exp(diff * diff * factor)
            diff = column - pos_ref[v, 1:2, at] * (PC - 1.0)
            col_ref[v, :, at] = jnp.exp(diff * diff * factor).astype(jnp.bfloat16)


def degrid_kernel(bands, mix_ref, lane_ref, col_ref, row_ref, sub_ref, swap_ref, *refs):
    band_refs, own_ref, out_ref = refs[: bands - 1], refs[bands - 1], refs[bands]
    height = 2 * CR
    share_rows = CAP * height
    core = lax.axis_index("facet") % 2
    parts = [jnp.where(core == 0, sub_ref[:share_rows], swap_ref[:share_rows])]
    own_ref[...] = parts[0]
    for k in range(1, bands):
        at = pl.ds((k - 1) * share_rows, share_rows)
        parts.append(jnp.where(core == 0, swap_ref[at], band_refs[k - 1][share_rows:]))
    held = [
        part[c * height : (c + 1) * height].astype(jnp.float32) for part in parts for c in range(CAP)
    ]
    for v in range(col_ref.shape[0]):
        halves = []
        for first in (0, HALF):
            mixed = None
            for i, sub in enumerate(held):
                share = jnp.concatenate([mix_ref[v, i]] * (height // 8), axis=0)
                part = sub[:, first : first + HALF] * share
                mixed = part if mixed is None else mixed + part
            halves.append(mixed)
        lane = lane_ref[v]
        within = lax.rem(lane, HALF)
        near, far = (jnp.take_along_axis(half, within, axis=1, mode="promise_in_bounds") for half in halves)
        patch = jnp.where(lane < HALF, near, far)
        partial = jnp.dot(
            patch.astype(jnp.bfloat16), col_ref[v], preferred_element_type=jnp.float32
        )
        out_ref[v, 0:1, :] = jnp.sum(partial[:CR] * row_ref[v], axis=0, keepdims=True)
        out_ref[v, 1:2, :] = jnp.sum(partial[CR:] * row_ref[v], axis=0, keepdims=True)


def local(
    facets, col_window, slot_of_subgrid, block_slot, block_band, block_offset, block_weight, vis_pos
):
    facet_count = lax.axis_size("facet")
    band_count = lax.axis_size("band")
    chips = facet_count // 2
    strip_rows = facets.shape[3]
    length = facets.shape[4]
    sky_rows = facet_count * strip_rows
    blocks, points = vis_pos.shape[2], vis_pos.shape[4]
    share_rows = CAP * 2 * CR
    height = 2 * share_rows
    chunks = 4
    core = lax.axis_index("facet") % 2

    def swap(x):
        return lax.ppermute(x, "facet", [(i, i ^ 1) for i in range(facet_count)])

    strip = facets.reshape(2 * strip_rows, length)
    table = jnp.asarray(column_map(length, SG))
    term_shape = jax.ShapeDtypeStruct((height, SG), jnp.bfloat16)
    spectrum, phases = pl.pallas_call(
        functools.partial(front_kernel, sky_rows, chunks),
        out_shape=(
            jax.ShapeDtypeStruct((2 * strip_rows, SG), jnp.bfloat16),
            jax.ShapeDtypeStruct(((chips - 1) * height, 4 * strip_rows), jnp.bfloat16),
        ),
        in_specs=[HBM] * 4,
        out_specs=(VMEM,) * 2,
        scratch_shapes=[
            pltpu.VMEM((2 * strip_rows, length), jnp.bfloat16),
            pltpu.VMEM((length // 2, 2 * SG), jnp.bfloat16),
            pltpu.VMEM((1, length), jnp.float32),
            pltpu.SMEM(slot_of_subgrid.shape, jnp.int32),
            pltpu.SemaphoreType.DMA((2 * chunks,)),
            pltpu.SemaphoreType.DMA((chunks,)),
            pltpu.SemaphoreType.DMA((2,)),
            pltpu.SMEM((facet_count * CAP,), jnp.int32),
        ],
        compiler_params=pltpu.CompilerParams(vmem_limit_bytes=32 * 2**20),
        name="front",
    )(*(
        pltpu.with_memory_space_constraint(x, pltpu.HBM)
        for x in (slot_of_subgrid, strip, col_window.reshape(1, length), table)
    ))

    other = swap(spectrum)
    terms = pl.pallas_call(
        functools.partial(term_kernel, 1.0 / math.sqrt(sky_rows)),
        out_shape=(term_shape,) * (chips - 1),
        in_specs=[VMEM] * 3,
        out_specs=(VMEM,) * (chips - 1),
        compiler_params=pltpu.CompilerParams(vmem_limit_bytes=16 * 2**20),
        name="terms",
    )(phases, spectrum, other)
    arrived = [
        lax.ppermute(
            terms[k - 1],
            "facet",
            [
                (i, 2 * send_to(k, i // 2, chips) if i % 2 else i + 1)
                for i in range(facet_count)
            ],
        )
        for k in range(1, chips)
    ]
    total = terms[0].astype(jnp.float32)
    for part in arrived:
        total = total + part.astype(jnp.float32)
    chip_subs = total.astype(jnp.bfloat16)

    col_kernel, row_kernel, mix, lanes, core_map = pl.pallas_call(
        functools.partial(weights_kernel, band_count),
        out_shape=(
            jax.ShapeDtypeStruct((blocks, PC, points), jnp.bfloat16),
            jax.ShapeDtypeStruct((blocks, CR, points), jnp.float32),
            jax.ShapeDtypeStruct((blocks, band_count * CAP, 8, 128), jnp.float32),
            jax.ShapeDtypeStruct((blocks, 2 * CR, PC), jnp.int32),
            jax.ShapeDtypeStruct((8, SG), jnp.int32),
        ),
        in_specs=[SMEM] * 4 + [VMEM] * 2,
        out_specs=(VMEM,) * 5,
        compiler_params=pltpu.CompilerParams(vmem_limit_bytes=16 * 2**20),
        cost_estimate=pl.CostEstimate(
            flops=8 * blocks * PC * points, bytes_accessed=0, transcendentals=blocks * PC * points
        ),
        name="weights",
    )(
        block_slot.reshape(blocks), block_band.reshape(blocks), block_offset.reshape(blocks),
        block_weight.reshape(blocks), vis_pos.reshape(blocks, 2, points),
        chip_subs,
    )

    device = lambda band, facet: band * facet_count + facet
    band_subs = [
        lax.ppermute(
            chip_subs,
            ("band", "facet"),
            [
                (device(b, f), device(b, f - 1) if f % 2 else device(send_to(k, b, band_count), f + 1))
                for b in range(band_count)
                for f in range(facet_count)
            ],
        )
        for k in range(1, band_count)
    ]
    for_other = jnp.where(
        core_map[:1] == 0,
        jnp.concatenate([chip_subs[share_rows:]] * (band_count - 1)),
        jnp.concatenate([part[:share_rows] for part in band_subs]),
    )
    from_other = swap(for_other)
    owned, visible = pl.pallas_call(
        functools.partial(degrid_kernel, band_count),
        out_shape=(
            jax.ShapeDtypeStruct((share_rows, SG), jnp.bfloat16),
            jax.ShapeDtypeStruct((blocks, 2, points), jnp.float32),
        ),
        in_specs=[VMEM] * (5 + band_count),
        out_specs=(VMEM,) * 2,
        compiler_params=pltpu.CompilerParams(vmem_limit_bytes=24 * 2**20),
        name="degrid",
    )(mix, lanes, col_kernel, row_kernel, chip_subs, from_other, *band_subs)
    return (
        owned.reshape(1, CAP, 2, CR, SG),
        visible.reshape(1, 1, blocks, 2, points),
    )


def solution(mesh):
    in_specs = (
        P("band", "facet", None, None, None),
        P(),
        P(),
        P("band", "facet", None),
        P("band", "facet", None),
        P("band", "facet", None),
        P("band", "facet", None),
        P("band", "facet", None, None, None),
    )
    out_specs = (P("band", "facet", None, None, None), P("band", "facet", None, None, None))
    return jax.shard_map(local, mesh=mesh, in_specs=in_specs, out_specs=out_specs, check_vma=False)
```

```python
import functools
import math

import jax
import jax.numpy as jnp
import numpy as np
from jax import lax
from jax.experimental import pallas as pl
from jax.experimental.pallas import tpu as pltpu
from jax.sharding import PartitionSpec as P

SG = 256
CR = 16
CAP = 2
PC = 128
HALF = SG // 2

kernel_sigma = 1.5
VMEM = pl.BlockSpec(memory_space=pltpu.VMEM)
SMEM = pl.BlockSpec(memory_space=pltpu.SMEM)
HBM = pl.BlockSpec(memory_space=pltpu.HBM)


def send_to(k, i, n):
    return i ^ k if n & (n - 1) == 0 else (i + k) % n


def recv_from(k, i, n):
    return i ^ k if n & (n - 1) == 0 else (i - k + n) % n


def column_seed(length, width):
    ratio = length // width
    place = (ratio * np.arange(width // 2)[None, :] - np.arange(ratio)[:, None])[:, :, None]
    out = []
    for parity in (0, 1):
        freq = np.arange(parity, width, 2)
        both = np.exp(2j * np.pi / length * (place * freq % length)).sum(-1)
        both = both / math.sqrt(length) / math.sqrt(width)
        out += [both.real, both.imag]
    return np.concatenate(out, axis=0).astype(jnp.bfloat16)


def front_kernel(
    chunks, facets_ref, window_hbm, seed_hbm, spec_ref,
    strip, table, window_ref, seed_ref, strip_sems, small_sems
):
    rows, length = strip.shape
    half = length // 2
    width = half // chunks
    strip_rows = rows // 2
    seed_copy = pltpu.make_async_copy(seed_hbm, seed_ref, small_sems.at[0])
    window_copy = pltpu.make_async_copy(window_hbm, window_ref, small_sems.at[1])
    seed_copy.start()
    window_copy.start()
    copies = []
    for i in range(chunks):
        cols = pl.ds(i * width, width)
        upper = pl.ds(half + i * width, width)
        copies.append((
            pltpu.make_async_copy(facets_ref.at[:, cols], strip.at[:, cols], strip_sems.at[2 * i]),
            pltpu.make_async_copy(facets_ref.at[:, upper], strip.at[:, upper], strip_sems.at[2 * i + 1]),
        ))
    for group in copies:
        for copy in group:
            copy.start()

    seed_copy.wait()
    ratio = length // SG
    lane = lax.broadcasted_iota(jnp.int32, (ratio, HALF), 1)
    for a in range(HALF):
        turned = pltpu.roll(seed_ref[...], a, 1) if a else seed_ref[...]
        at = pl.ds(a * ratio, ratio)
        for kind in range(4):
            part = turned[kind * ratio : (kind + 1) * ratio]
            if kind >= 2 and a:
                part = jnp.where(lane < a, -part, part)
            table[at, kind * HALF : (kind + 1) * HALF] = part.astype(jnp.bfloat16)

    window_copy.wait()
    even = odd = None
    for i in range(chunks):
        for copy in copies[i]:
            copy.wait()
        cols = pl.ds(i * width, width)
        upper = pl.ds(half + i * width, width)
        near = strip[:, cols].astype(jnp.float32) * window_ref[:, cols]
        far = strip[:, upper].astype(jnp.float32) * window_ref[:, upper]
        even_part = jnp.dot(
            (near + far).astype(jnp.bfloat16), table[cols, :SG], preferred_element_type=jnp.float32
        )
        odd_part = jnp.dot(
            (near - far).astype(jnp.bfloat16), table[cols, SG:], preferred_element_type=jnp.float32
        )
        even = even_part if even is None else even + even_part
        odd = odd_part if odd is None else odd + odd_part
    n = strip_rows
    even_real = even[:n, :HALF] - even[n:, HALF:]
    even_imag = even[:n, HALF:] + even[n:, :HALF]
    odd_real = odd[:n, :HALF] - odd[n:, HALF:]
    odd_imag = odd[:n, HALF:] + odd[n:, :HALF]
    spec_ref[:n, :HALF] = (even_real + odd_real).astype(jnp.bfloat16)
    spec_ref[:n, HALF:] = (even_real - odd_real).astype(jnp.bfloat16)
    spec_ref[n:, :HALF] = (even_imag + odd_imag).astype(jnp.bfloat16)
    spec_ref[n:, HALF:] = (even_imag - odd_imag).astype(jnp.bfloat16)


def phase_kernel(total, slot_ref, spec_ref, phase_ref, partial_ref):
    strip_rows = spec_ref.shape[0] // 2
    slots = phase_ref.shape[0] // (2 * CR)
    chip_slots = 2 * CAP
    facet = lax.axis_index("facet")
    chips = lax.axis_size("facet") // 2
    chip = facet // 2
    core = facet % 2

    padded = -(-slots // 8) * 8
    number = lax.broadcasted_iota(jnp.int32, (padded, strip_rows), 0)
    message = number // chip_slots + 1
    owner = jnp.where(core == 0, chip, send_to(message, chip, chips))
    slot = owner * chip_slots + number % chip_slots
    subgrids = slot_ref.shape[1]
    match = slot[:, :subgrids] == slot_ref[...]
    order = lax.broadcasted_iota(jnp.int32, match.shape, 1).astype(jnp.float32) + 1.0
    found = jnp.sum(jnp.where(match, order, 0.0), axis=1, keepdims=True)
    live = jnp.broadcast_to(jnp.where(found > 0.0, 1.0, 0.0), (padded, strip_rows))
    first = jnp.broadcast_to(jnp.maximum(found - 1.0, 0.0).astype(jnp.int32) * CR, (padded, strip_rows))

    step = 2.0 * math.pi / total

    def turn(product):
        if total & (total - 1) == 0:
            product = product & (total - 1)
        else:
            product = lax.rem(product, total)
        angle = step * product.astype(jnp.float32)
        return jnp.cos(angle), jnp.sin(angle)

    lane = lax.broadcasted_iota(jnp.int32, (padded, strip_rows), 1)
    row = lax.broadcasted_iota(jnp.int32, (CR, strip_rows), 0)
    for side in range(2):
        cell = (facet if side == 0 else facet ^ 1) * strip_rows + lane
        row_cos, row_sin = turn(row * cell[:1])
        first_cos, first_sin = turn(first * cell)
        first_cos, first_sin = first_cos * live, first_sin * live
        left = pl.ds(2 * side * strip_rows, strip_rows)
        right = pl.ds((2 * side + 1) * strip_rows, strip_rows)
        for c in range(slots):
            base_cos, base_sin = first_cos[c : c + 1], first_sin[c : c + 1]
            cos = (base_cos * row_cos - base_sin * row_sin).astype(jnp.bfloat16)
            sin = (base_sin * row_cos + base_cos * row_sin).astype(jnp.bfloat16)
            at = c * 2 * CR
            phase_ref[pl.ds(at, CR), left] = cos
            phase_ref[pl.ds(at, CR), right] = sin
            phase_ref[pl.ds(at + CR, CR), left] = -sin
            phase_ref[pl.ds(at + CR, CR), right] = cos

    partial_ref[...] = jnp.dot(
        phase_ref[:, : 2 * strip_rows], spec_ref[...], preferred_element_type=jnp.float32
    )


def term_kernel(scale, phase_ref, partial_ref, other_ref, *out_refs):
    depth = other_ref.shape[0]
    height = out_refs[0].shape[0]

    def write_terms(count):
        rows = count * height
        terms = partial_ref[:rows] + jnp.dot(
            phase_ref[:rows, depth:], other_ref[...], preferred_element_type=jnp.float32
        )
        terms = (terms * scale).astype(jnp.bfloat16)
        for k in range(count):
            out_refs[k][...] = terms[k * height : (k + 1) * height]

    core = lax.axis_index("facet") % 2

    @pl.when(core == 0)
    def _():
        write_terms(1)

    @pl.when(core == 1)
    def _():
        write_terms(len(out_refs))


def weights_kernel(
    bands, slot_ref, band_ref, offset_ref, weight_ref, pos_ref, after_ref, col_ref, row_ref, mix_ref, lane_ref, core_ref
):
    blocks, width, points = col_ref.shape
    factor = -1.0 / (2.0 * kernel_sigma * kernel_sigma)
    tile = 512
    me = lax.axis_index("band")
    core_ref[...] = jnp.full(core_ref.shape, lax.axis_index("facet") % 2, jnp.int32)
    column = lax.broadcasted_iota(jnp.int32, (width, tile), 0).astype(jnp.float32)
    row = lax.broadcasted_iota(jnp.int32, (CR, tile), 0).astype(jnp.float32)
    for v in range(blocks):
        low = band_ref[v]
        slot = slot_ref[v]
        weight = weight_ref[v]
        for k in range(bands):
            band = recv_from(k, me, bands)
            share = jnp.where(band == low, 1.0 - weight, jnp.where(band == low + 1, weight, 0.0))
            for c in range(CAP):
                mix_ref[v, k * CAP + c] = jnp.full((8, 128), jnp.where(slot == c, share, 0.0), jnp.float32)
        lane_ref[v] = offset_ref[v] + lax.broadcasted_iota(jnp.int32, (2 * CR, PC), 1)
        for t in range(0, points, tile):
            at = pl.ds(t, tile)
            diff = row - pos_ref[v, 0:1, at] * (CR - 1.0)
            row_ref[v, :, at] = jnp.exp(diff * diff * factor)
            diff = column - pos_ref[v, 1:2, at] * (PC - 1.0)
            col_ref[v, :, at] = jnp.exp(diff * diff * factor).astype(jnp.bfloat16)


def degrid_kernel(bands, mix_ref, lane_ref, col_ref, row_ref, sub_ref, swap_ref, *refs):
    band_refs, own_ref, out_ref = refs[: bands - 1], refs[bands - 1], refs[bands]
    height = 2 * CR
    share_rows = CAP * height
    core = lax.axis_index("facet") % 2
    parts = [jnp.where(core == 0, sub_ref[:share_rows], swap_ref[:share_rows])]
    own_ref[...] = parts[0]
    for k in range(1, bands):
        at = pl.ds((k - 1) * share_rows, share_rows)
        parts.append(jnp.where(core == 0, swap_ref[at], band_refs[k - 1][share_rows:]))
    held = [
        part[c * height : (c + 1) * height].astype(jnp.float32) for part in parts for c in range(CAP)
    ]
    for v in range(col_ref.shape[0]):
        halves = []
        for first in (0, HALF):
            mixed = None
            for i, sub in enumerate(held):
                share = jnp.concatenate([mix_ref[v, i]] * (height // 8), axis=0)
                part = sub[:, first : first + HALF] * share
                mixed = part if mixed is None else mixed + part
            halves.append(mixed)
        lane = lane_ref[v]
        within = lax.rem(lane, HALF)
        near, far = (jnp.take_along_axis(half, within, axis=1, mode="promise_in_bounds") for half in halves)
        patch = jnp.where(lane < HALF, near, far)
        partial = jnp.dot(
            patch.astype(jnp.bfloat16), col_ref[v], preferred_element_type=jnp.float32
        )
        out_ref[v, 0:1, :] = jnp.sum(partial[:CR] * row_ref[v], axis=0, keepdims=True)
        out_ref[v, 1:2, :] = jnp.sum(partial[CR:] * row_ref[v], axis=0, keepdims=True)


def local(
    facets, col_window, slot_of_subgrid, block_slot, block_band, block_offset, block_weight, vis_pos
):
    facet_count = lax.axis_size("facet")
    band_count = lax.axis_size("band")
    chips = facet_count // 2
    strip_rows = facets.shape[3]
    length = facets.shape[4]
    sky_rows = facet_count * strip_rows
    blocks, points = vis_pos.shape[2], vis_pos.shape[4]
    share_rows = CAP * 2 * CR
    height = 2 * share_rows
    chunks = 1
    core = lax.axis_index("facet") % 2

    def swap(x):
        return lax.ppermute(x, "facet", [(i, i ^ 1) for i in range(facet_count)])

    strip = facets.reshape(2 * strip_rows, length)
    seed = jnp.asarray(column_seed(length, SG))
    term_shape = jax.ShapeDtypeStruct((height, SG), jnp.bfloat16)
    spectrum = pl.pallas_call(
        functools.partial(front_kernel, chunks),
        out_shape=jax.ShapeDtypeStruct((2 * strip_rows, SG), jnp.bfloat16),
        in_specs=[HBM] * 3,
        out_specs=VMEM,
        scratch_shapes=[
            pltpu.VMEM((2 * strip_rows, length), jnp.bfloat16),
            pltpu.VMEM((length // 2, 2 * SG), jnp.bfloat16),
            pltpu.VMEM((1, length), jnp.float32),
            pltpu.VMEM(seed.shape, seed.dtype),
            pltpu.SemaphoreType.DMA((2 * chunks,)),
            pltpu.SemaphoreType.DMA((2,)),
        ],
        compiler_params=pltpu.CompilerParams(vmem_limit_bytes=32 * 2**20),
        name="front",
    )(*(
        pltpu.with_memory_space_constraint(x, pltpu.HBM)
        for x in (strip, col_window.reshape(1, length), seed)
    ))

    other = swap(spectrum)
    phase_rows = (chips - 1) * height
    phases, partial = pl.pallas_call(
        functools.partial(phase_kernel, sky_rows),
        out_shape=(
            jax.ShapeDtypeStruct((phase_rows, 4 * strip_rows), jnp.bfloat16),
            jax.ShapeDtypeStruct((phase_rows, SG), jnp.float32),
        ),
        in_specs=[VMEM] * 2,
        out_specs=(VMEM,) * 2,
        compiler_params=pltpu.CompilerParams(vmem_limit_bytes=32 * 2**20),
        name="phases",
    )(slot_of_subgrid.reshape(1, -1), spectrum)
    terms = pl.pallas_call(
        functools.partial(term_kernel, 1.0 / math.sqrt(sky_rows)),
        out_shape=(term_shape,) * (chips - 1),
        in_specs=[VMEM] * 3,
        out_specs=(VMEM,) * (chips - 1),
        compiler_params=pltpu.CompilerParams(vmem_limit_bytes=16 * 2**20),
        name="terms",
    )(phases, partial, other)
    arrived = [
        lax.ppermute(
            terms[k - 1],
            "facet",
            [
                (i, 2 * send_to(k, i // 2, chips) if i % 2 else i + 1)
                for i in range(facet_count)
            ],
        )
        for k in range(1, chips)
    ]
    total = terms[0].astype(jnp.float32)
    for part in arrived:
        total = total + part.astype(jnp.float32)
    chip_subs = total.astype(jnp.bfloat16)

    col_kernel, row_kernel, mix, lanes, core_map = pl.pallas_call(
        functools.partial(weights_kernel, band_count),
        out_shape=(
            jax.ShapeDtypeStruct((blocks, PC, points), jnp.bfloat16),
            jax.ShapeDtypeStruct((blocks, CR, points), jnp.float32),
            jax.ShapeDtypeStruct((blocks, band_count * CAP, 8, 128), jnp.float32),
            jax.ShapeDtypeStruct((blocks, 2 * CR, PC), jnp.int32),
            jax.ShapeDtypeStruct((8, SG), jnp.int32),
        ),
        in_specs=[SMEM] * 4 + [VMEM] * 2,
        out_specs=(VMEM,) * 5,
        compiler_params=pltpu.CompilerParams(vmem_limit_bytes=16 * 2**20),
        cost_estimate=pl.CostEstimate(
            flops=8 * blocks * PC * points, bytes_accessed=0, transcendentals=blocks * PC * points
        ),
        name="weights",
    )(
        block_slot.reshape(blocks), block_band.reshape(blocks), block_offset.reshape(blocks),
        block_weight.reshape(blocks), vis_pos.reshape(blocks, 2, points),
        chip_subs,
    )

    device = lambda band, facet: band * facet_count + facet
    band_subs = [
        lax.ppermute(
            chip_subs,
            ("band", "facet"),
            [
                (device(b, f), device(b, f - 1) if f % 2 else device(send_to(k, b, band_count), f + 1))
                for b in range(band_count)
                for f in range(facet_count)
            ],
        )
        for k in range(1, band_count)
    ]
    for_other = jnp.where(
        core_map[:1] == 0,
        jnp.concatenate([chip_subs[share_rows:]] * (band_count - 1)),
        jnp.concatenate([part[:share_rows] for part in band_subs]),
    )
    from_other = swap(for_other)
    owned, visible = pl.pallas_call(
        functools.partial(degrid_kernel, band_count),
        out_shape=(
            jax.ShapeDtypeStruct((share_rows, SG), jnp.bfloat16),
            jax.ShapeDtypeStruct((blocks, 2, points), jnp.float32),
        ),
        in_specs=[VMEM] * (5 + band_count),
        out_specs=(VMEM,) * 2,
        compiler_params=pltpu.CompilerParams(vmem_limit_bytes=24 * 2**20),
        name="degrid",
    )(mix, lanes, col_kernel, row_kernel, chip_subs, from_other, *band_subs)
    return (
        owned.reshape(1, CAP, 2, CR, SG),
        visible.reshape(1, 1, blocks, 2, points),
    )


def solution(mesh):
    in_specs = (
        P("band", "facet", None, None, None),
        P(),
        P(),
        P("band", "facet", None),
        P("band", "facet", None),
        P("band", "facet", None),
        P("band", "facet", None),
        P("band", "facet", None, None, None),
    )
    out_specs = (P("band", "facet", None, None, None), P("band", "facet", None, None, None))
    return jax.shard_map(local, mesh=mesh, in_specs=in_specs, out_specs=out_specs, check_vma=False)
```

```python
import functools
import math

import jax
import jax.numpy as jnp
import numpy as np
from jax import lax
from jax.experimental import pallas as pl
from jax.experimental.pallas import tpu as pltpu
from jax.sharding import PartitionSpec as P

SG = 256
CR = 16
CAP = 2
PC = 128
HALF = SG // 2

kernel_sigma = 1.5
VMEM = pl.BlockSpec(memory_space=pltpu.VMEM)
SMEM = pl.BlockSpec(memory_space=pltpu.SMEM)
HBM = pl.BlockSpec(memory_space=pltpu.HBM)


def chip_to(k, i, n):
    return i ^ k if n & (n - 1) == 0 else (i + k) % n


def band_to(k, i, n):
    return (i + k) % n


def band_from(k, i, n):
    return (i - k + n) % n


def column_seed(length, width):
    ratio = length // width
    place = (ratio * np.arange(width // 2)[None, :] - np.arange(ratio)[:, None])[:, :, None]
    out = []
    for parity in (0, 1):
        freq = np.arange(parity, width, 2)
        both = np.exp(2j * np.pi / length * (place * freq % length)).sum(-1)
        both = both / math.sqrt(length) / math.sqrt(width)
        out += [both.real, both.imag]
    return np.concatenate(out, axis=0).astype(jnp.bfloat16)


def front_kernel(
    chunks, facets_ref, window_hbm, seed_hbm, spec_ref,
    strip, table, window_ref, seed_ref, strip_sems, small_sems
):
    rows, length = strip.shape
    half = length // 2
    width = half // chunks
    strip_rows = rows // 2
    seed_copy = pltpu.make_async_copy(seed_hbm, seed_ref, small_sems.at[0])
    window_copy = pltpu.make_async_copy(window_hbm, window_ref, small_sems.at[1])
    seed_copy.start()
    window_copy.start()
    copies = []
    for i in range(chunks):
        cols = pl.ds(i * width, width)
        upper = pl.ds(half + i * width, width)
        copies.append((
            pltpu.make_async_copy(facets_ref.at[:, cols], strip.at[:, cols], strip_sems.at[2 * i]),
            pltpu.make_async_copy(facets_ref.at[:, upper], strip.at[:, upper], strip_sems.at[2 * i + 1]),
        ))
    for group in copies:
        for copy in group:
            copy.start()

    seed_copy.wait()
    ratio = length // SG
    lane = lax.broadcasted_iota(jnp.int32, (ratio, HALF), 1)
    for a in range(HALF):
        turned = pltpu.roll(seed_ref[...], a, 1) if a else seed_ref[...]
        at = pl.ds(a * ratio, ratio)
        for kind in range(4):
            part = turned[kind * ratio : (kind + 1) * ratio]
            if kind >= 2 and a:
                part = jnp.where(lane < a, -part, part)
            table[at, kind * HALF : (kind + 1) * HALF] = part.astype(jnp.bfloat16)

    window_copy.wait()
    even = odd = None
    for i in range(chunks):
        for copy in copies[i]:
            copy.wait()
        cols = pl.ds(i * width, width)
        upper = pl.ds(half + i * width, width)
        near = strip[:, cols].astype(jnp.float32) * window_ref[:, cols]
        far = strip[:, upper].astype(jnp.float32) * window_ref[:, upper]
        even_part = jnp.dot(
            (near + far).astype(jnp.bfloat16), table[cols, :SG], preferred_element_type=jnp.float32
        )
        odd_part = jnp.dot(
            (near - far).astype(jnp.bfloat16), table[cols, SG:], preferred_element_type=jnp.float32
        )
        even = even_part if even is None else even + even_part
        odd = odd_part if odd is None else odd + odd_part
    n = strip_rows
    even_real = even[:n, :HALF] - even[n:, HALF:]
    even_imag = even[:n, HALF:] + even[n:, :HALF]
    odd_real = odd[:n, :HALF] - odd[n:, HALF:]
    odd_imag = odd[:n, HALF:] + odd[n:, :HALF]
    spec_ref[:n, :HALF] = (even_real + odd_real).astype(jnp.bfloat16)
    spec_ref[:n, HALF:] = (even_real - odd_real).astype(jnp.bfloat16)
    spec_ref[n:, :HALF] = (even_imag + odd_imag).astype(jnp.bfloat16)
    spec_ref[n:, HALF:] = (even_imag - odd_imag).astype(jnp.bfloat16)


def phase_kernel(total, slot_ref, spec_ref, phase_ref, partial_ref):
    strip_rows = spec_ref.shape[0] // 2
    slots = phase_ref.shape[0] // (2 * CR)
    chip_slots = 2 * CAP
    facet = lax.axis_index("facet")
    chips = lax.axis_size("facet") // 2
    chip = facet // 2
    core = facet % 2

    padded = -(-slots // 8) * 8
    number = lax.broadcasted_iota(jnp.int32, (padded, strip_rows), 0)
    message = number // chip_slots + 1
    owner = jnp.where(core == 0, chip, chip_to(message, chip, chips))
    slot = owner * chip_slots + number % chip_slots
    subgrids = slot_ref.shape[1]
    match = slot[:, :subgrids] == slot_ref[...]
    order = lax.broadcasted_iota(jnp.int32, match.shape, 1).astype(jnp.float32) + 1.0
    found = jnp.sum(jnp.where(match, order, 0.0), axis=1, keepdims=True)
    live = jnp.broadcast_to(jnp.where(found > 0.0, 1.0, 0.0), (padded, strip_rows))
    first = jnp.broadcast_to(jnp.maximum(found - 1.0, 0.0).astype(jnp.int32) * CR, (padded, strip_rows))

    step = 2.0 * math.pi / total

    def turn(product):
        if total & (total - 1) == 0:
            product = product & (total - 1)
        else:
            product = lax.rem(product, total)
        angle = step * product.astype(jnp.float32)
        return jnp.cos(angle), jnp.sin(angle)

    lane = lax.broadcasted_iota(jnp.int32, (padded, strip_rows), 1)
    row = lax.broadcasted_iota(jnp.int32, (CR, strip_rows), 0)
    for side in range(2):
        cell = (facet if side == 0 else facet ^ 1) * strip_rows + lane
        row_cos, row_sin = turn(row * cell[:1])
        first_cos, first_sin = turn(first * cell)
        first_cos, first_sin = first_cos * live, first_sin * live
        left = pl.ds(2 * side * strip_rows, strip_rows)
        right = pl.ds((2 * side + 1) * strip_rows, strip_rows)
        for c in range(slots):
            base_cos, base_sin = first_cos[c : c + 1], first_sin[c : c + 1]
            cos = (base_cos * row_cos - base_sin * row_sin).astype(jnp.bfloat16)
            sin = (base_sin * row_cos + base_cos * row_sin).astype(jnp.bfloat16)
            at = c * 2 * CR
            phase_ref[pl.ds(at, CR), left] = cos
            phase_ref[pl.ds(at, CR), right] = sin
            phase_ref[pl.ds(at + CR, CR), left] = -sin
            phase_ref[pl.ds(at + CR, CR), right] = cos

    partial_ref[...] = jnp.dot(
        phase_ref[:, : 2 * strip_rows], spec_ref[...], preferred_element_type=jnp.float32
    )


def term_kernel(scale, phase_ref, partial_ref, other_ref, *out_refs):
    depth = other_ref.shape[0]
    height = out_refs[0].shape[0]

    def write_terms(count):
        rows = count * height
        terms = partial_ref[:rows] + jnp.dot(
            phase_ref[:rows, depth:], other_ref[...], preferred_element_type=jnp.float32
        )
        terms = (terms * scale).astype(jnp.bfloat16)
        for k in range(count):
            out_refs[k][...] = terms[k * height : (k + 1) * height]

    core = lax.axis_index("facet") % 2

    @pl.when(core == 0)
    def _():
        write_terms(1)

    @pl.when(core == 1)
    def _():
        write_terms(len(out_refs))


def weights_kernel(
    bands, slot_ref, band_ref, offset_ref, weight_ref, pos_ref, after_ref, col_ref, row_ref, mix_ref, lane_ref, core_ref
):
    blocks, width, points = col_ref.shape
    factor = -1.0 / (2.0 * kernel_sigma * kernel_sigma)
    tile = 512
    me = lax.axis_index("band")
    core_ref[...] = jnp.full(core_ref.shape, lax.axis_index("facet") % 2, jnp.int32)
    column = lax.broadcasted_iota(jnp.int32, (width, tile), 0).astype(jnp.float32)
    row = lax.broadcasted_iota(jnp.int32, (CR, tile), 0).astype(jnp.float32)
    for v in range(blocks):
        low = band_ref[v]
        slot = slot_ref[v]
        weight = weight_ref[v]
        for k in range(bands):
            band = band_from(k, me, bands)
            share = jnp.where(band == low, 1.0 - weight, jnp.where(band == low + 1, weight, 0.0))
            for c in range(CAP):
                mix_ref[v, k * CAP + c] = jnp.full((8, 128), jnp.where(slot == c, share, 0.0), jnp.float32)
        lane_ref[v] = offset_ref[v] + lax.broadcasted_iota(jnp.int32, (2 * CR, PC), 1)
        for t in range(0, points, tile):
            at = pl.ds(t, tile)
            diff = row - pos_ref[v, 0:1, at] * (CR - 1.0)
            row_ref[v, :, at] = jnp.exp(diff * diff * factor)
            diff = column - pos_ref[v, 1:2, at] * (PC - 1.0)
            col_ref[v, :, at] = jnp.exp(diff * diff * factor).astype(jnp.bfloat16)


def degrid_kernel(bands, mix_ref, lane_ref, col_ref, row_ref, sub_ref, swap_ref, *refs):
    band_refs, own_ref, out_ref = refs[: bands - 1], refs[bands - 1], refs[bands]
    height = 2 * CR
    share_rows = CAP * height
    core = lax.axis_index("facet") % 2
    parts = [jnp.where(core == 0, sub_ref[:share_rows], swap_ref[:share_rows])]
    own_ref[...] = parts[0]
    for k in range(1, bands):
        at = pl.ds((bands - 1 - k) * share_rows, share_rows)
        parts.append(jnp.where(core == 0, swap_ref[at], band_refs[bands - 1 - k][share_rows:]))
    held = [
        part[c * height : (c + 1) * height].astype(jnp.float32) for part in parts for c in range(CAP)
    ]
    for v in range(col_ref.shape[0]):
        halves = []
        for first in (0, HALF):
            mixed = None
            for i, sub in enumerate(held):
                share = jnp.concatenate([mix_ref[v, i]] * (height // 8), axis=0)
                part = sub[:, first : first + HALF] * share
                mixed = part if mixed is None else mixed + part
            halves.append(mixed)
        lane = lane_ref[v]
        within = lax.rem(lane, HALF)
        near, far = (jnp.take_along_axis(half, within, axis=1, mode="promise_in_bounds") for half in halves)
        patch = jnp.where(lane < HALF, near, far)
        partial = jnp.dot(
            patch.astype(jnp.bfloat16), col_ref[v], preferred_element_type=jnp.float32
        )
        out_ref[v, 0:1, :] = jnp.sum(partial[:CR] * row_ref[v], axis=0, keepdims=True)
        out_ref[v, 1:2, :] = jnp.sum(partial[CR:] * row_ref[v], axis=0, keepdims=True)


def local(
    facets, col_window, slot_of_subgrid, block_slot, block_band, block_offset, block_weight, vis_pos
):
    facet_count = lax.axis_size("facet")
    band_count = lax.axis_size("band")
    chips = facet_count // 2
    strip_rows = facets.shape[3]
    length = facets.shape[4]
    sky_rows = facet_count * strip_rows
    blocks, points = vis_pos.shape[2], vis_pos.shape[4]
    share_rows = CAP * 2 * CR
    height = 2 * share_rows
    chunks = 1
    core = lax.axis_index("facet") % 2

    def swap(x):
        return lax.ppermute(x, "facet", [(i, i ^ 1) for i in range(facet_count)])

    strip = facets.reshape(2 * strip_rows, length)
    seed = jnp.asarray(column_seed(length, SG))
    term_shape = jax.ShapeDtypeStruct((height, SG), jnp.bfloat16)
    spectrum = pl.pallas_call(
        functools.partial(front_kernel, chunks),
        out_shape=jax.ShapeDtypeStruct((2 * strip_rows, SG), jnp.bfloat16),
        in_specs=[HBM] * 3,
        out_specs=VMEM,
        scratch_shapes=[
            pltpu.VMEM((2 * strip_rows, length), jnp.bfloat16),
            pltpu.VMEM((length // 2, 2 * SG), jnp.bfloat16),
            pltpu.VMEM((1, length), jnp.float32),
            pltpu.VMEM(seed.shape, seed.dtype),
            pltpu.SemaphoreType.DMA((2 * chunks,)),
            pltpu.SemaphoreType.DMA((2,)),
        ],
        compiler_params=pltpu.CompilerParams(vmem_limit_bytes=32 * 2**20),
        name="front",
    )(*(
        pltpu.with_memory_space_constraint(x, pltpu.HBM)
        for x in (strip, col_window.reshape(1, length), seed)
    ))

    other = swap(spectrum)
    phase_rows = (chips - 1) * height
    phases, partial = pl.pallas_call(
        functools.partial(phase_kernel, sky_rows),
        out_shape=(
            jax.ShapeDtypeStruct((phase_rows, 4 * strip_rows), jnp.bfloat16),
            jax.ShapeDtypeStruct((phase_rows, SG), jnp.float32),
        ),
        in_specs=[VMEM] * 2,
        out_specs=(VMEM,) * 2,
        compiler_params=pltpu.CompilerParams(vmem_limit_bytes=32 * 2**20),
        name="phases",
    )(slot_of_subgrid.reshape(1, -1), spectrum)
    terms = pl.pallas_call(
        functools.partial(term_kernel, 1.0 / math.sqrt(sky_rows)),
        out_shape=(term_shape,) * (chips - 1),
        in_specs=[VMEM] * 3,
        out_specs=(VMEM,) * (chips - 1),
        compiler_params=pltpu.CompilerParams(vmem_limit_bytes=16 * 2**20),
        name="terms",
    )(phases, partial, other)
    arrived = [
        lax.ppermute(
            terms[k - 1],
            "facet",
            [
                (i, 2 * chip_to(k, i // 2, chips) if i % 2 else i + 1)
                for i in range(facet_count)
            ],
        )
        for k in range(1, chips)
    ]
    total = terms[0].astype(jnp.float32)
    for part in arrived:
        total = total + part.astype(jnp.float32)
    chip_subs = total.astype(jnp.bfloat16)

    col_kernel, row_kernel, mix, lanes, core_map = pl.pallas_call(
        functools.partial(weights_kernel, band_count),
        out_shape=(
            jax.ShapeDtypeStruct((blocks, PC, points), jnp.bfloat16),
            jax.ShapeDtypeStruct((blocks, CR, points), jnp.float32),
            jax.ShapeDtypeStruct((blocks, band_count * CAP, 8, 128), jnp.float32),
            jax.ShapeDtypeStruct((blocks, 2 * CR, PC), jnp.int32),
            jax.ShapeDtypeStruct((8, SG), jnp.int32),
        ),
        in_specs=[SMEM] * 4 + [VMEM] * 2,
        out_specs=(VMEM,) * 5,
        compiler_params=pltpu.CompilerParams(vmem_limit_bytes=16 * 2**20),
        cost_estimate=pl.CostEstimate(
            flops=8 * blocks * PC * points, bytes_accessed=0, transcendentals=blocks * PC * points
        ),
        name="weights",
    )(
        block_slot.reshape(blocks), block_band.reshape(blocks), block_offset.reshape(blocks),
        block_weight.reshape(blocks), vis_pos.reshape(blocks, 2, points),
        chip_subs,
    )

    device = lambda band, facet: band * facet_count + facet
    band_subs = [
        lax.ppermute(
            chip_subs,
            ("band", "facet"),
            [
                (device(b, f), device(b, f - 1) if f % 2 else device(band_to(k, b, band_count), f + 1))
                for b in range(band_count)
                for f in range(facet_count)
            ],
        )
        for k in range(1, band_count)
    ][::-1]
    for_other = jnp.where(
        core_map[:1] == 0,
        jnp.concatenate([chip_subs[share_rows:]] * (band_count - 1)),
        jnp.concatenate([part[:share_rows] for part in band_subs]),
    )
    from_other = swap(for_other)
    owned, visible = pl.pallas_call(
        functools.partial(degrid_kernel, band_count),
        out_shape=(
            jax.ShapeDtypeStruct((share_rows, SG), jnp.bfloat16),
            jax.ShapeDtypeStruct((blocks, 2, points), jnp.float32),
        ),
        in_specs=[VMEM] * (5 + band_count),
        out_specs=(VMEM,) * 2,
        compiler_params=pltpu.CompilerParams(vmem_limit_bytes=24 * 2**20),
        name="degrid",
    )(mix, lanes, col_kernel, row_kernel, chip_subs, from_other, *band_subs)
    return (
        owned.reshape(1, CAP, 2, CR, SG),
        visible.reshape(1, 1, blocks, 2, points),
    )


def solution(mesh):
    in_specs = (
        P("band", "facet", None, None, None),
        P(),
        P(),
        P("band", "facet", None),
        P("band", "facet", None),
        P("band", "facet", None),
        P("band", "facet", None),
        P("band", "facet", None, None, None),
    )
    out_specs = (P("band", "facet", None, None, None), P("band", "facet", None, None, None))
    return jax.shard_map(local, mesh=mesh, in_specs=in_specs, out_specs=out_specs, check_vma=False)
```

```python
import functools
import math

import jax
import jax.numpy as jnp
import numpy as np
from jax import lax
from jax.experimental import pallas as pl
from jax.experimental.pallas import tpu as pltpu
from jax.sharding import PartitionSpec as P

SG = 256
CR = 16
CAP = 2
PC = 128
HALF = SG // 2

kernel_sigma = 1.5
VMEM = pl.BlockSpec(memory_space=pltpu.VMEM)
SMEM = pl.BlockSpec(memory_space=pltpu.SMEM)
HBM = pl.BlockSpec(memory_space=pltpu.HBM)


def chip_to(k, i, n):
    return i ^ k if n & (n - 1) == 0 else (i + k) % n


def band_to(k, i, n):
    return (i + k) % n


def band_from(k, i, n):
    return (i - k + n) % n


def column_seed(length, width):
    ratio = length // width
    place = (ratio * np.arange(width // 2)[None, :] - np.arange(ratio)[:, None])[:, :, None]
    out = []
    for parity in (0, 1):
        freq = np.arange(parity, width, 2)
        both = np.exp(2j * np.pi / length * (place * freq % length)).sum(-1)
        both = both / math.sqrt(length) / math.sqrt(width)
        out += [both.real, both.imag]
    return np.concatenate(out, axis=0).astype(jnp.bfloat16)


def front_kernel(
    chunks, facets_ref, window_hbm, seed_hbm, spec_ref,
    strip, table, window_ref, seed_ref, strip_sems, small_sems
):
    rows, length = strip.shape
    half = length // 2
    width = half // chunks
    strip_rows = rows // 2
    seed_copy = pltpu.make_async_copy(seed_hbm, seed_ref, small_sems.at[0])
    window_copy = pltpu.make_async_copy(window_hbm, window_ref, small_sems.at[1])
    seed_copy.start()
    window_copy.start()
    copies = []
    for i in range(chunks):
        cols = pl.ds(i * width, width)
        upper = pl.ds(half + i * width, width)
        copies.append((
            pltpu.make_async_copy(facets_ref.at[:, cols], strip.at[:, cols], strip_sems.at[2 * i]),
            pltpu.make_async_copy(facets_ref.at[:, upper], strip.at[:, upper], strip_sems.at[2 * i + 1]),
        ))
    for group in copies:
        for copy in group:
            copy.start()

    seed_copy.wait()
    ratio = length // SG
    lane = lax.broadcasted_iota(jnp.int32, (ratio, HALF), 1)
    for a in range(HALF):
        turned = pltpu.roll(seed_ref[...], a, 1) if a else seed_ref[...]
        at = pl.ds(a * ratio, ratio)
        for kind in range(4):
            part = turned[kind * ratio : (kind + 1) * ratio]
            if kind >= 2 and a:
                part = jnp.where(lane < a, -part, part)
            table[at, kind * HALF : (kind + 1) * HALF] = part.astype(jnp.bfloat16)

    window_copy.wait()
    even = odd = None
    for i in range(chunks):
        for copy in copies[i]:
            copy.wait()
        cols = pl.ds(i * width, width)
        upper = pl.ds(half + i * width, width)
        near = strip[:, cols].astype(jnp.float32) * window_ref[:, cols]
        far = strip[:, upper].astype(jnp.float32) * window_ref[:, upper]
        even_part = jnp.dot(
            (near + far).astype(jnp.bfloat16), table[cols, :SG], preferred_element_type=jnp.float32
        )
        odd_part = jnp.dot(
            (near - far).astype(jnp.bfloat16), table[cols, SG:], preferred_element_type=jnp.float32
        )
        even = even_part if even is None else even + even_part
        odd = odd_part if odd is None else odd + odd_part
    n = strip_rows
    even_real = even[:n, :HALF] - even[n:, HALF:]
    even_imag = even[:n, HALF:] + even[n:, :HALF]
    odd_real = odd[:n, :HALF] - odd[n:, HALF:]
    odd_imag = odd[:n, HALF:] + odd[n:, :HALF]
    spec_ref[:n, :HALF] = (even_real + odd_real).astype(jnp.bfloat16)
    spec_ref[:n, HALF:] = (even_real - odd_real).astype(jnp.bfloat16)
    spec_ref[n:, :HALF] = (even_imag + odd_imag).astype(jnp.bfloat16)
    spec_ref[n:, HALF:] = (even_imag - odd_imag).astype(jnp.bfloat16)


def phase_kernel(total, slot_ref, spec_ref, phase_ref, partial_ref):
    strip_rows = spec_ref.shape[0] // 2
    slots = phase_ref.shape[0] // (2 * CR)
    chip_slots = 2 * CAP
    facet = lax.axis_index("facet")
    chips = lax.axis_size("facet") // 2
    chip = facet // 2
    core = facet % 2

    padded = -(-slots // 8) * 8
    number = lax.broadcasted_iota(jnp.int32, (padded, strip_rows), 0)
    message = number // chip_slots + 1
    owner = jnp.where(core == 0, chip, chip_to(message, chip, chips))
    slot = owner * chip_slots + number % chip_slots
    subgrids = slot_ref.shape[1]
    match = slot[:, :subgrids] == slot_ref[...]
    order = lax.broadcasted_iota(jnp.int32, match.shape, 1).astype(jnp.float32) + 1.0
    found = jnp.sum(jnp.where(match, order, 0.0), axis=1, keepdims=True)
    live = jnp.broadcast_to(jnp.where(found > 0.0, 1.0, 0.0), (padded, strip_rows))
    first = jnp.broadcast_to(jnp.maximum(found - 1.0, 0.0).astype(jnp.int32) * CR, (padded, strip_rows))

    step = 2.0 * math.pi / total

    def turn(product):
        if total & (total - 1) == 0:
            product = product & (total - 1)
        else:
            product = lax.rem(product, total)
        angle = step * product.astype(jnp.float32)
        return jnp.cos(angle), jnp.sin(angle)

    lane = lax.broadcasted_iota(jnp.int32, (padded, strip_rows), 1)
    row = lax.broadcasted_iota(jnp.int32, (CR, strip_rows), 0)
    for side in range(2):
        cell = (facet if side == 0 else facet ^ 1) * strip_rows + lane
        row_cos, row_sin = turn(row * cell[:1])
        first_cos, first_sin = turn(first * cell)
        first_cos, first_sin = first_cos * live, first_sin * live
        left = pl.ds(2 * side * strip_rows, strip_rows)
        right = pl.ds((2 * side + 1) * strip_rows, strip_rows)
        for c in range(slots):
            base_cos, base_sin = first_cos[c : c + 1], first_sin[c : c + 1]
            cos = (base_cos * row_cos - base_sin * row_sin).astype(jnp.bfloat16)
            sin = (base_sin * row_cos + base_cos * row_sin).astype(jnp.bfloat16)
            at = c * 2 * CR
            phase_ref[pl.ds(at, CR), left] = cos
            phase_ref[pl.ds(at, CR), right] = sin
            phase_ref[pl.ds(at + CR, CR), left] = -sin
            phase_ref[pl.ds(at + CR, CR), right] = cos

    partial_ref[...] = jnp.dot(
        phase_ref[:, : 2 * strip_rows], spec_ref[...], preferred_element_type=jnp.float32
    )


def term_kernel(core, first, scale, phase_ref, partial_ref, other_ref, *out_refs):
    depth = other_ref.shape[0]
    height = out_refs[0].shape[0]
    rows = slice(first * height, (first + len(out_refs)) * height)

    @pl.when(lax.axis_index("facet") % 2 == core)
    def _():
        terms = partial_ref[rows] + jnp.dot(
            phase_ref[rows, depth:], other_ref[...], preferred_element_type=jnp.float32
        )
        terms = (terms * scale).astype(jnp.bfloat16)
        for k, out_ref in enumerate(out_refs):
            out_ref[...] = terms[k * height : (k + 1) * height]


def weights_kernel(
    bands, slot_hbm, band_hbm, offset_hbm, weight_hbm, pos_hbm, after_ref, col_ref, row_ref, mix_ref,
    lane_ref, core_ref, slot_ref, band_ref, offset_ref, weight_ref, pos_ref, sems
):
    pairs = [
        (slot_hbm, slot_ref), (band_hbm, band_ref), (offset_hbm, offset_ref),
        (weight_hbm, weight_ref), (pos_hbm, pos_ref),
    ]
    copies = [pltpu.make_async_copy(a, b, sems.at[i]) for i, (a, b) in enumerate(pairs)]
    for copy in copies:
        copy.start()
    for copy in copies:
        copy.wait()
    blocks, width, points = col_ref.shape
    factor = -1.0 / (2.0 * kernel_sigma * kernel_sigma)
    tile = 512
    me = lax.axis_index("band")
    core_ref[...] = jnp.full(core_ref.shape, lax.axis_index("facet") % 2, jnp.int32)
    column = lax.broadcasted_iota(jnp.int32, (width, tile), 0).astype(jnp.float32)
    row = lax.broadcasted_iota(jnp.int32, (CR, tile), 0).astype(jnp.float32)
    for v in range(blocks):
        low = band_ref[v]
        slot = slot_ref[v]
        weight = weight_ref[v]
        for k in range(bands):
            band = band_from(k, me, bands)
            share = jnp.where(band == low, 1.0 - weight, jnp.where(band == low + 1, weight, 0.0))
            for c in range(CAP):
                mix_ref[v, k * CAP + c] = jnp.full((8, 128), jnp.where(slot == c, share, 0.0), jnp.float32)
        lane_ref[v] = offset_ref[v] + lax.broadcasted_iota(jnp.int32, (2 * CR, PC), 1)
        for t in range(0, points, tile):
            at = pl.ds(t, tile)
            diff = row - pos_ref[v, 0:1, at] * (CR - 1.0)
            row_ref[v, :, at] = jnp.exp(diff * diff * factor)
            diff = column - pos_ref[v, 1:2, at] * (PC - 1.0)
            col_ref[v, :, at] = jnp.exp(diff * diff * factor).astype(jnp.bfloat16)


def degrid_kernel(bands, mix_ref, lane_ref, col_ref, row_ref, sub_ref, swap_ref, *refs):
    band_refs, own_ref, out_ref = refs[: bands - 1], refs[bands - 1], refs[bands]
    height = 2 * CR
    share_rows = CAP * height
    core = lax.axis_index("facet") % 2
    parts = [jnp.where(core == 0, sub_ref[:share_rows], swap_ref[:share_rows])]
    own_ref[...] = parts[0]
    for k in range(1, bands):
        at = pl.ds((bands - 1 - k) * share_rows, share_rows)
        parts.append(jnp.where(core == 0, swap_ref[at], band_refs[bands - 1 - k][share_rows:]))
    held = [
        part[c * height : (c + 1) * height].astype(jnp.float32) for part in parts for c in range(CAP)
    ]
    for v in range(col_ref.shape[0]):
        halves = []
        for first in (0, HALF):
            mixed = None
            for i, sub in enumerate(held):
                share = jnp.concatenate([mix_ref[v, i]] * (height // 8), axis=0)
                part = sub[:, first : first + HALF] * share
                mixed = part if mixed is None else mixed + part
            halves.append(mixed)
        lane = lane_ref[v]
        within = lax.rem(lane, HALF)
        near, far = (jnp.take_along_axis(half, within, axis=1, mode="promise_in_bounds") for half in halves)
        patch = jnp.where(lane < HALF, near, far)
        partial = jnp.dot(
            patch.astype(jnp.bfloat16), col_ref[v], preferred_element_type=jnp.float32
        )
        out_ref[v, 0:1, :] = jnp.sum(partial[:CR] * row_ref[v], axis=0, keepdims=True)
        out_ref[v, 1:2, :] = jnp.sum(partial[CR:] * row_ref[v], axis=0, keepdims=True)


def local(
    facets, col_window, slot_of_subgrid, block_slot, block_band, block_offset, block_weight, vis_pos
):
    facet_count = lax.axis_size("facet")
    band_count = lax.axis_size("band")
    chips = facet_count // 2
    strip_rows = facets.shape[3]
    length = facets.shape[4]
    sky_rows = facet_count * strip_rows
    blocks, points = vis_pos.shape[2], vis_pos.shape[4]
    share_rows = CAP * 2 * CR
    height = 2 * share_rows
    chunks = 1
    core = lax.axis_index("facet") % 2

    def swap(x):
        return lax.ppermute(x, "facet", [(i, i ^ 1) for i in range(facet_count)])

    strip = facets.reshape(2 * strip_rows, length)
    seed = jnp.asarray(column_seed(length, SG))
    term_shape = jax.ShapeDtypeStruct((height, SG), jnp.bfloat16)
    spectrum = pl.pallas_call(
        functools.partial(front_kernel, chunks),
        out_shape=jax.ShapeDtypeStruct((2 * strip_rows, SG), jnp.bfloat16),
        in_specs=[HBM] * 3,
        out_specs=VMEM,
        scratch_shapes=[
            pltpu.VMEM((2 * strip_rows, length), jnp.bfloat16),
            pltpu.VMEM((length // 2, 2 * SG), jnp.bfloat16),
            pltpu.VMEM((1, length), jnp.float32),
            pltpu.VMEM(seed.shape, seed.dtype),
            pltpu.SemaphoreType.DMA((2 * chunks,)),
            pltpu.SemaphoreType.DMA((2,)),
        ],
        compiler_params=pltpu.CompilerParams(vmem_limit_bytes=32 * 2**20),
        name="front",
    )(*(
        pltpu.with_memory_space_constraint(x, pltpu.HBM)
        for x in (strip, col_window.reshape(1, length), seed)
    ))

    other = swap(spectrum)
    phase_rows = (chips - 1) * height
    phases, partial = pl.pallas_call(
        functools.partial(phase_kernel, sky_rows),
        out_shape=(
            jax.ShapeDtypeStruct((phase_rows, 4 * strip_rows), jnp.bfloat16),
            jax.ShapeDtypeStruct((phase_rows, SG), jnp.float32),
        ),
        in_specs=[VMEM] * 2,
        out_specs=(VMEM,) * 2,
        compiler_params=pltpu.CompilerParams(vmem_limit_bytes=32 * 2**20),
        name="phases",
    )(slot_of_subgrid.reshape(1, -1), spectrum)
    def make_terms(core, first, chip_count, name):
        return pl.pallas_call(
            functools.partial(term_kernel, core, first, 1.0 / math.sqrt(sky_rows)),
            out_shape=(term_shape,) * chip_count,
            in_specs=[VMEM] * 3,
            out_specs=(VMEM,) * chip_count,
            compiler_params=pltpu.CompilerParams(vmem_limit_bytes=16 * 2**20),
            name=name,
        )(phases, partial, other)

    terms = [make_terms(1, k - 1, 1, "terms")[0] for k in range(1, chips)]
    (own_terms,) = make_terms(0, 0, 1, "own_terms")
    arrived = [
        lax.ppermute(
            terms[k - 1],
            "facet",
            [
                (i, 2 * chip_to(k, i // 2, chips) if i % 2 else i + 1)
                for i in range(facet_count)
            ],
        )
        for k in range(1, chips)
    ]
    total = own_terms.astype(jnp.float32)
    for part in [arrived[k - 1] for k in (2, 3, 1)]:
        total = total + part.astype(jnp.float32)
    chip_subs = total.astype(jnp.bfloat16)

    col_kernel, row_kernel, mix, lanes, core_map = pl.pallas_call(
        functools.partial(weights_kernel, band_count),
        out_shape=(
            jax.ShapeDtypeStruct((blocks, PC, points), jnp.bfloat16),
            jax.ShapeDtypeStruct((blocks, CR, points), jnp.float32),
            jax.ShapeDtypeStruct((blocks, band_count * CAP, 8, 128), jnp.float32),
            jax.ShapeDtypeStruct((blocks, 2 * CR, PC), jnp.int32),
            jax.ShapeDtypeStruct((8, SG), jnp.int32),
        ),
        in_specs=[HBM] * 5 + [VMEM],
        out_specs=(VMEM,) * 5,
        scratch_shapes=[
            pltpu.SMEM((blocks,), jnp.int32),
            pltpu.SMEM((blocks,), jnp.int32),
            pltpu.SMEM((blocks,), jnp.int32),
            pltpu.SMEM((blocks,), jnp.float32),
            pltpu.VMEM((blocks, 2, points), jnp.float32),
            pltpu.SemaphoreType.DMA((5,)),
        ],
        compiler_params=pltpu.CompilerParams(vmem_limit_bytes=16 * 2**20),
        cost_estimate=pl.CostEstimate(
            flops=8 * blocks * PC * points, bytes_accessed=0, transcendentals=blocks * PC * points
        ),
        name="weights",
    )(
        *(
            pltpu.with_memory_space_constraint(x, pltpu.HBM)
            for x in (
                block_slot.reshape(blocks), block_band.reshape(blocks), block_offset.reshape(blocks),
                block_weight.reshape(blocks), vis_pos.reshape(blocks, 2, points),
            )
        ),
        chip_subs,
    )

    device = lambda band, facet: band * facet_count + facet
    band_subs = [
        lax.ppermute(
            chip_subs,
            ("band", "facet"),
            [
                (device(b, f), device(b, f - 1) if f % 2 else device(band_to(k, b, band_count), f + 1))
                for b in range(band_count)
                for f in range(facet_count)
            ],
        )
        for k in range(1, band_count)
    ][::-1]
    for_other = jnp.where(
        core_map[:1] == 0,
        jnp.concatenate([chip_subs[share_rows:]] * (band_count - 1)),
        jnp.concatenate([part[:share_rows] for part in band_subs]),
    )
    from_other = swap(for_other)
    owned, visible = pl.pallas_call(
        functools.partial(degrid_kernel, band_count),
        out_shape=(
            jax.ShapeDtypeStruct((share_rows, SG), jnp.bfloat16),
            jax.ShapeDtypeStruct((blocks, 2, points), jnp.float32),
        ),
        in_specs=[VMEM] * (5 + band_count),
        out_specs=(VMEM,) * 2,
        compiler_params=pltpu.CompilerParams(vmem_limit_bytes=24 * 2**20),
        name="degrid",
    )(mix, lanes, col_kernel, row_kernel, chip_subs, from_other, *band_subs)
    return (
        owned.reshape(1, CAP, 2, CR, SG),
        visible.reshape(1, 1, blocks, 2, points),
    )


def solution(mesh):
    in_specs = (
        P("band", "facet", None, None, None),
        P(),
        P(),
        P("band", "facet", None),
        P("band", "facet", None),
        P("band", "facet", None),
        P("band", "facet", None),
        P("band", "facet", None, None, None),
    )
    out_specs = (P("band", "facet", None, None, None), P("band", "facet", None, None, None))
    return jax.shard_map(local, mesh=mesh, in_specs=in_specs, out_specs=out_specs, check_vma=False)
```

```python
import functools
import math

import jax
import jax.numpy as jnp
import numpy as np
from jax import lax
from jax.experimental import pallas as pl
from jax.experimental.pallas import tpu as pltpu
from jax.sharding import PartitionSpec as P

SG = 256
CR = 16
CAP = 2
PC = 128
HALF = SG // 2

kernel_sigma = 1.5
VMEM = pl.BlockSpec(memory_space=pltpu.VMEM)
SMEM = pl.BlockSpec(memory_space=pltpu.SMEM)
HBM = pl.BlockSpec(memory_space=pltpu.HBM)


def chip_to(k, i, n):
    return i ^ k if n & (n - 1) == 0 else (i + k) % n


def band_to(k, i, n):
    return (i + k) % n


def band_from(k, i, n):
    return (i - k + n) % n


def column_seed(length, width):
    ratio = length // width
    place = (ratio * np.arange(width // 2)[None, :] - np.arange(ratio)[:, None])[:, :, None]
    out = []
    for parity in (0, 1):
        freq = np.arange(parity, width, 2)
        both = np.exp(2j * np.pi / length * (place * freq % length)).sum(-1)
        both = both / math.sqrt(length) / math.sqrt(width)
        out += [both.real, both.imag]
    return np.concatenate(out, axis=0).astype(jnp.bfloat16)


def front_kernel(
    chunks, facets_ref, window_hbm, seed_hbm, spec_ref,
    strip, table, window_ref, seed_ref, strip_sems, small_sems
):
    rows, length = strip.shape
    half = length // 2
    width = half // chunks
    strip_rows = rows // 2
    seed_copy = pltpu.make_async_copy(seed_hbm, seed_ref, small_sems.at[0])
    window_copy = pltpu.make_async_copy(window_hbm, window_ref, small_sems.at[1])
    seed_copy.start()
    window_copy.start()
    copies = []
    for i in range(chunks):
        cols = pl.ds(i * width, width)
        upper = pl.ds(half + i * width, width)
        copies.append((
            pltpu.make_async_copy(facets_ref.at[:, cols], strip.at[:, cols], strip_sems.at[2 * i]),
            pltpu.make_async_copy(facets_ref.at[:, upper], strip.at[:, upper], strip_sems.at[2 * i + 1]),
        ))
    for group in copies:
        for copy in group:
            copy.start()

    seed_copy.wait()
    ratio = length // SG
    lane = lax.broadcasted_iota(jnp.int32, (ratio, HALF), 1)
    for a in range(HALF):
        turned = pltpu.roll(seed_ref[...], a, 1) if a else seed_ref[...]
        at = pl.ds(a * ratio, ratio)
        for kind in range(4):
            part = turned[kind * ratio : (kind + 1) * ratio]
            if kind >= 2 and a:
                part = jnp.where(lane < a, -part, part)
            table[at, kind * HALF : (kind + 1) * HALF] = part.astype(jnp.bfloat16)

    window_copy.wait()
    even = odd = None
    for i in range(chunks):
        for copy in copies[i]:
            copy.wait()
        cols = pl.ds(i * width, width)
        upper = pl.ds(half + i * width, width)
        near = strip[:, cols].astype(jnp.float32) * window_ref[:, cols]
        far = strip[:, upper].astype(jnp.float32) * window_ref[:, upper]
        even_part = jnp.dot(
            (near + far).astype(jnp.bfloat16), table[cols, :SG], preferred_element_type=jnp.float32
        )
        odd_part = jnp.dot(
            (near - far).astype(jnp.bfloat16), table[cols, SG:], preferred_element_type=jnp.float32
        )
        even = even_part if even is None else even + even_part
        odd = odd_part if odd is None else odd + odd_part
    n = strip_rows
    even_real = even[:n, :HALF] - even[n:, HALF:]
    even_imag = even[:n, HALF:] + even[n:, :HALF]
    odd_real = odd[:n, :HALF] - odd[n:, HALF:]
    odd_imag = odd[:n, HALF:] + odd[n:, :HALF]
    spec_ref[:n, :HALF] = (even_real + odd_real).astype(jnp.bfloat16)
    spec_ref[:n, HALF:] = (even_real - odd_real).astype(jnp.bfloat16)
    spec_ref[n:, :HALF] = (even_imag + odd_imag).astype(jnp.bfloat16)
    spec_ref[n:, HALF:] = (even_imag - odd_imag).astype(jnp.bfloat16)


def phase_kernel(total, slot_ref, spec_ref, phase_ref, partial_ref):
    strip_rows = spec_ref.shape[0] // 2
    slots = phase_ref.shape[0] // (2 * CR)
    chip_slots = 2 * CAP
    facet = lax.axis_index("facet")
    chips = lax.axis_size("facet") // 2
    chip = facet // 2
    core = facet % 2

    padded = -(-slots // 8) * 8
    number = lax.broadcasted_iota(jnp.int32, (padded, strip_rows), 0)
    message = number // chip_slots + 1
    owner = jnp.where(core == 0, chip, chip_to(message, chip, chips))
    slot = owner * chip_slots + number % chip_slots
    subgrids = slot_ref.shape[1]
    match = slot[:, :subgrids] == slot_ref[...]
    order = lax.broadcasted_iota(jnp.int32, match.shape, 1).astype(jnp.float32) + 1.0
    found = jnp.sum(jnp.where(match, order, 0.0), axis=1, keepdims=True)
    live = jnp.broadcast_to(jnp.where(found > 0.0, 1.0, 0.0), (padded, strip_rows))
    first = jnp.broadcast_to(jnp.maximum(found - 1.0, 0.0).astype(jnp.int32) * CR, (padded, strip_rows))

    step = 2.0 * math.pi / total

    def turn(product):
        if total & (total - 1) == 0:
            product = product & (total - 1)
        else:
            product = lax.rem(product, total)
        angle = step * product.astype(jnp.float32)
        return jnp.cos(angle), jnp.sin(angle)

    lane = lax.broadcasted_iota(jnp.int32, (padded, strip_rows), 1)
    row = lax.broadcasted_iota(jnp.int32, (CR, strip_rows), 0)
    for side in range(2):
        cell = (facet if side == 0 else facet ^ 1) * strip_rows + lane
        row_cos, row_sin = turn(row * cell[:1])
        first_cos, first_sin = turn(first * cell)
        first_cos, first_sin = first_cos * live, first_sin * live
        left = pl.ds(2 * side * strip_rows, strip_rows)
        right = pl.ds((2 * side + 1) * strip_rows, strip_rows)
        for c in range(slots):
            base_cos, base_sin = first_cos[c : c + 1], first_sin[c : c + 1]
            cos = (base_cos * row_cos - base_sin * row_sin).astype(jnp.bfloat16)
            sin = (base_sin * row_cos + base_cos * row_sin).astype(jnp.bfloat16)
            at = c * 2 * CR
            phase_ref[pl.ds(at, CR), left] = cos
            phase_ref[pl.ds(at, CR), right] = sin
            phase_ref[pl.ds(at + CR, CR), left] = -sin
            phase_ref[pl.ds(at + CR, CR), right] = cos

    partial_ref[...] = jnp.dot(
        phase_ref[:, : 2 * strip_rows], spec_ref[...], preferred_element_type=jnp.float32
    )


def term_kernel(core, first, scale, phase_ref, partial_ref, other_ref, *out_refs):
    depth = other_ref.shape[0]
    height = out_refs[0].shape[0]
    rows = slice(first * height, (first + len(out_refs)) * height)

    @pl.when(lax.axis_index("facet") % 2 == core)
    def _():
        terms = partial_ref[rows] + jnp.dot(
            phase_ref[rows, depth:], other_ref[...], preferred_element_type=jnp.float32
        )
        terms = (terms * scale).astype(jnp.bfloat16)
        for k, out_ref in enumerate(out_refs):
            out_ref[...] = terms[k * height : (k + 1) * height]


def weights_kernel(
    bands, slot_hbm, band_hbm, offset_hbm, weight_hbm, pos_hbm, after_ref, col_ref, row_ref, mix_ref,
    lane_ref, core_ref, slot_ref, band_ref, offset_ref, weight_ref, pos_ref, sems
):
    pairs = [
        (slot_hbm, slot_ref), (band_hbm, band_ref), (offset_hbm, offset_ref),
        (weight_hbm, weight_ref), (pos_hbm, pos_ref),
    ]
    copies = [pltpu.make_async_copy(a, b, sems.at[i]) for i, (a, b) in enumerate(pairs)]
    for copy in copies:
        copy.start()
    for copy in copies:
        copy.wait()
    blocks, width, points = col_ref.shape
    factor = -1.0 / (2.0 * kernel_sigma * kernel_sigma)
    tile = 512
    me = lax.axis_index("band")
    core_ref[...] = jnp.full(core_ref.shape, lax.axis_index("facet") % 2, jnp.int32)
    column = lax.broadcasted_iota(jnp.int32, (width, tile), 0).astype(jnp.float32)
    row = lax.broadcasted_iota(jnp.int32, (CR, tile), 0).astype(jnp.float32)
    for v in range(blocks):
        low = band_ref[v]
        slot = slot_ref[v]
        weight = weight_ref[v]
        for k in range(bands):
            band = band_from(k, me, bands)
            share = jnp.where(band == low, 1.0 - weight, jnp.where(band == low + 1, weight, 0.0))
            for c in range(CAP):
                mix_ref[v, k * CAP + c] = jnp.full((8, 128), jnp.where(slot == c, share, 0.0), jnp.float32)
        lane_ref[v] = offset_ref[v] + lax.broadcasted_iota(jnp.int32, (2 * CR, PC), 1)
        for t in range(0, points, tile):
            at = pl.ds(t, tile)
            diff = row - pos_ref[v, 0:1, at] * (CR - 1.0)
            row_ref[v, :, at] = jnp.exp(diff * diff * factor)
            diff = column - pos_ref[v, 1:2, at] * (PC - 1.0)
            col_ref[v, :, at] = jnp.exp(diff * diff * factor).astype(jnp.bfloat16)


def degrid_kernel(bands, mix_ref, lane_ref, col_ref, row_ref, sub_ref, swap_ref, *refs):
    band_refs, own_ref, out_ref = refs[: bands - 1], refs[bands - 1], refs[bands]
    height = 2 * CR
    share_rows = CAP * height
    core = lax.axis_index("facet") % 2
    parts = [jnp.where(core == 0, sub_ref[:share_rows], swap_ref[:share_rows])]
    own_ref[...] = parts[0]
    for k in range(1, bands):
        at = pl.ds((bands - 1 - k) * share_rows, share_rows)
        parts.append(jnp.where(core == 0, swap_ref[at], band_refs[bands - 1 - k][share_rows:]))
    held = [
        part[c * height : (c + 1) * height].astype(jnp.float32) for part in parts for c in range(CAP)
    ]
    for v in range(col_ref.shape[0]):
        halves = []
        for first in (0, HALF):
            mixed = None
            for i, sub in enumerate(held):
                share = jnp.concatenate([mix_ref[v, i]] * (height // 8), axis=0)
                part = sub[:, first : first + HALF] * share
                mixed = part if mixed is None else mixed + part
            halves.append(mixed)
        lane = lane_ref[v]
        within = lax.rem(lane, HALF)
        near, far = (jnp.take_along_axis(half, within, axis=1, mode="promise_in_bounds") for half in halves)
        patch = jnp.where(lane < HALF, near, far)
        partial = jnp.dot(
            patch.astype(jnp.bfloat16), col_ref[v], preferred_element_type=jnp.float32
        )
        out_ref[v, 0:1, :] = jnp.sum(partial[:CR] * row_ref[v], axis=0, keepdims=True)
        out_ref[v, 1:2, :] = jnp.sum(partial[CR:] * row_ref[v], axis=0, keepdims=True)


def local(
    facets, col_window, slot_of_subgrid, block_slot, block_band, block_offset, block_weight, vis_pos
):
    facet_count = lax.axis_size("facet")
    band_count = lax.axis_size("band")
    chips = facet_count // 2
    strip_rows = facets.shape[3]
    length = facets.shape[4]
    sky_rows = facet_count * strip_rows
    blocks, points = vis_pos.shape[2], vis_pos.shape[4]
    share_rows = CAP * 2 * CR
    height = 2 * share_rows
    chunks = 1
    core = lax.axis_index("facet") % 2

    def swap(x):
        return lax.ppermute(x, "facet", [(i, i ^ 1) for i in range(facet_count)])

    strip = facets.reshape(2 * strip_rows, length)
    seed = jnp.asarray(column_seed(length, SG))
    term_shape = jax.ShapeDtypeStruct((height, SG), jnp.bfloat16)
    spectrum = pl.pallas_call(
        functools.partial(front_kernel, chunks),
        out_shape=jax.ShapeDtypeStruct((2 * strip_rows, SG), jnp.bfloat16),
        in_specs=[HBM] * 3,
        out_specs=VMEM,
        scratch_shapes=[
            pltpu.VMEM((2 * strip_rows, length), jnp.bfloat16),
            pltpu.VMEM((length // 2, 2 * SG), jnp.bfloat16),
            pltpu.VMEM((1, length), jnp.float32),
            pltpu.VMEM(seed.shape, seed.dtype),
            pltpu.SemaphoreType.DMA((2 * chunks,)),
            pltpu.SemaphoreType.DMA((2,)),
        ],
        compiler_params=pltpu.CompilerParams(vmem_limit_bytes=32 * 2**20),
        name="front",
    )(*(
        pltpu.with_memory_space_constraint(x, pltpu.HBM)
        for x in (strip, col_window.reshape(1, length), seed)
    ))

    other = swap(spectrum)
    phase_rows = (chips - 1) * height
    phases, partial = pl.pallas_call(
        functools.partial(phase_kernel, sky_rows),
        out_shape=(
            jax.ShapeDtypeStruct((phase_rows, 4 * strip_rows), jnp.bfloat16),
            jax.ShapeDtypeStruct((phase_rows, SG), jnp.float32),
        ),
        in_specs=[VMEM] * 2,
        out_specs=(VMEM,) * 2,
        compiler_params=pltpu.CompilerParams(vmem_limit_bytes=32 * 2**20),
        name="phases",
    )(slot_of_subgrid.reshape(1, -1), spectrum)
    def make_terms(core, first, chip_count, name):
        return pl.pallas_call(
            functools.partial(term_kernel, core, first, 1.0 / math.sqrt(sky_rows)),
            out_shape=(term_shape,) * chip_count,
            in_specs=[VMEM] * 3,
            out_specs=(VMEM,) * chip_count,
            compiler_params=pltpu.CompilerParams(vmem_limit_bytes=16 * 2**20),
            name=name,
        )(phases, partial, other)

    terms = [make_terms(1, k - 1, 1, "terms")[0] for k in range(1, chips)]
    (own_terms,) = make_terms(0, 0, 1, "own_terms")
    arrived = [
        lax.ppermute(
            terms[k - 1],
            "facet",
            [
                (i, 2 * chip_to(k, i // 2, chips) if i % 2 else i + 1)
                for i in range(facet_count)
            ],
        )
        for k in range(1, chips)
    ]
    total = own_terms.astype(jnp.float32)
    for part in arrived[1:] + arrived[:1]:
        total = total + part.astype(jnp.float32)
    chip_subs = total.astype(jnp.bfloat16)

    col_kernel, row_kernel, mix, lanes, core_map = pl.pallas_call(
        functools.partial(weights_kernel, band_count),
        out_shape=(
            jax.ShapeDtypeStruct((blocks, PC, points), jnp.bfloat16),
            jax.ShapeDtypeStruct((blocks, CR, points), jnp.float32),
            jax.ShapeDtypeStruct((blocks, band_count * CAP, 8, 128), jnp.float32),
            jax.ShapeDtypeStruct((blocks, 2 * CR, PC), jnp.int32),
            jax.ShapeDtypeStruct((8, SG), jnp.int32),
        ),
        in_specs=[HBM] * 5 + [VMEM],
        out_specs=(VMEM,) * 5,
        scratch_shapes=[
            pltpu.SMEM((blocks,), jnp.int32),
            pltpu.SMEM((blocks,), jnp.int32),
            pltpu.SMEM((blocks,), jnp.int32),
            pltpu.SMEM((blocks,), jnp.float32),
            pltpu.VMEM((blocks, 2, points), jnp.float32),
            pltpu.SemaphoreType.DMA((5,)),
        ],
        compiler_params=pltpu.CompilerParams(vmem_limit_bytes=16 * 2**20),
        cost_estimate=pl.CostEstimate(
            flops=8 * blocks * PC * points, bytes_accessed=0, transcendentals=blocks * PC * points
        ),
        name="weights",
    )(
        *(
            pltpu.with_memory_space_constraint(x, pltpu.HBM)
            for x in (
                block_slot.reshape(blocks), block_band.reshape(blocks), block_offset.reshape(blocks),
                block_weight.reshape(blocks), vis_pos.reshape(blocks, 2, points),
            )
        ),
        chip_subs,
    )

    device = lambda band, facet: band * facet_count + facet
    band_subs = [
        lax.ppermute(
            chip_subs,
            ("band", "facet"),
            [
                (device(b, f), device(b, f - 1) if f % 2 else device(band_to(k, b, band_count), f + 1))
                for b in range(band_count)
                for f in range(facet_count)
            ],
        )
        for k in range(1, band_count)
    ][::-1]
    for_other = jnp.where(
        core_map[:1] == 0,
        jnp.concatenate([chip_subs[share_rows:]] * (band_count - 1)),
        jnp.concatenate([part[:share_rows] for part in band_subs]),
    )
    from_other = swap(for_other)
    owned, visible = pl.pallas_call(
        functools.partial(degrid_kernel, band_count),
        out_shape=(
            jax.ShapeDtypeStruct((share_rows, SG), jnp.bfloat16),
            jax.ShapeDtypeStruct((blocks, 2, points), jnp.float32),
        ),
        in_specs=[VMEM] * (5 + band_count),
        out_specs=(VMEM,) * 2,
        compiler_params=pltpu.CompilerParams(vmem_limit_bytes=24 * 2**20),
        name="degrid",
    )(mix, lanes, col_kernel, row_kernel, chip_subs, from_other, *band_subs)
    return (
        owned.reshape(1, CAP, 2, CR, SG),
        visible.reshape(1, 1, blocks, 2, points),
    )


def solution(mesh):
    in_specs = (
        P("band", "facet", None, None, None),
        P(),
        P(),
        P("band", "facet", None),
        P("band", "facet", None),
        P("band", "facet", None),
        P("band", "facet", None),
        P("band", "facet", None, None, None),
    )
    out_specs = (P("band", "facet", None, None, None), P("band", "facet", None, None, None))
    return jax.shard_map(local, mesh=mesh, in_specs=in_specs, out_specs=out_specs, check_vma=False)
```

```python
import functools
import math

import jax
import jax.numpy as jnp
import numpy as np
from jax import lax
from jax.experimental import pallas as pl
from jax.experimental.pallas import tpu as pltpu
from jax.sharding import PartitionSpec as P

SG = 256
CR = 16
CAP = 2
PC = 128
HALF = SG // 2

kernel_sigma = 1.5
VMEM = pl.BlockSpec(memory_space=pltpu.VMEM)
SMEM = pl.BlockSpec(memory_space=pltpu.SMEM)
HBM = pl.BlockSpec(memory_space=pltpu.HBM)


def chip_to(k, i, n):
    return i ^ k if n & (n - 1) == 0 else (i + k) % n


def band_to(k, i, n):
    return (i + k) % n


def band_from(k, i, n):
    return (i - k + n) % n


def band_order(n):
    return list(range(n - 1, 2, -1)) + [k for k in (1, 2) if k < n]


def column_seed(length, width):
    ratio = length // width
    place = (ratio * np.arange(width // 2)[None, :] - np.arange(ratio)[:, None])[:, :, None]
    out = []
    for parity in (0, 1):
        freq = np.arange(parity, width, 2)
        both = np.exp(2j * np.pi / length * (place * freq % length)).sum(-1)
        both = both / math.sqrt(length) / math.sqrt(width)
        out += [both.real, both.imag]
    return np.concatenate(out, axis=0).astype(jnp.bfloat16)


def front_kernel(
    chunks, facets_ref, window_hbm, seed_hbm, spec_ref,
    strip, table, window_ref, seed_ref, strip_sems, small_sems
):
    rows, length = strip.shape
    half = length // 2
    width = half // chunks
    strip_rows = rows // 2
    seed_copy = pltpu.make_async_copy(seed_hbm, seed_ref, small_sems.at[0])
    window_copy = pltpu.make_async_copy(window_hbm, window_ref, small_sems.at[1])
    seed_copy.start()
    window_copy.start()
    copies = []
    for i in range(chunks):
        cols = pl.ds(i * width, width)
        upper = pl.ds(half + i * width, width)
        copies.append((
            pltpu.make_async_copy(facets_ref.at[:, cols], strip.at[:, cols], strip_sems.at[2 * i]),
            pltpu.make_async_copy(facets_ref.at[:, upper], strip.at[:, upper], strip_sems.at[2 * i + 1]),
        ))
    for group in copies:
        for copy in group:
            copy.start()

    seed_copy.wait()
    ratio = length // SG
    lane = lax.broadcasted_iota(jnp.int32, (ratio, HALF), 1)
    for a in range(HALF):
        turned = pltpu.roll(seed_ref[...], a, 1) if a else seed_ref[...]
        at = pl.ds(a * ratio, ratio)
        for kind in range(4):
            part = turned[kind * ratio : (kind + 1) * ratio]
            if kind >= 2 and a:
                part = jnp.where(lane < a, -part, part)
            table[at, kind * HALF : (kind + 1) * HALF] = part.astype(jnp.bfloat16)

    window_copy.wait()
    even = odd = None
    for i in range(chunks):
        for copy in copies[i]:
            copy.wait()
        cols = pl.ds(i * width, width)
        upper = pl.ds(half + i * width, width)
        near = strip[:, cols].astype(jnp.float32) * window_ref[:, cols]
        far = strip[:, upper].astype(jnp.float32) * window_ref[:, upper]
        even_part = jnp.dot(
            (near + far).astype(jnp.bfloat16), table[cols, :SG], preferred_element_type=jnp.float32
        )
        odd_part = jnp.dot(
            (near - far).astype(jnp.bfloat16), table[cols, SG:], preferred_element_type=jnp.float32
        )
        even = even_part if even is None else even + even_part
        odd = odd_part if odd is None else odd + odd_part
    n = strip_rows
    even_real = even[:n, :HALF] - even[n:, HALF:]
    even_imag = even[:n, HALF:] + even[n:, :HALF]
    odd_real = odd[:n, :HALF] - odd[n:, HALF:]
    odd_imag = odd[:n, HALF:] + odd[n:, :HALF]
    spec_ref[:n, :HALF] = (even_real + odd_real).astype(jnp.bfloat16)
    spec_ref[:n, HALF:] = (even_real - odd_real).astype(jnp.bfloat16)
    spec_ref[n:, :HALF] = (even_imag + odd_imag).astype(jnp.bfloat16)
    spec_ref[n:, HALF:] = (even_imag - odd_imag).astype(jnp.bfloat16)


def phase_kernel(total, slot_ref, spec_ref, phase_ref, partial_ref):
    strip_rows = spec_ref.shape[0] // 2
    slots = phase_ref.shape[0] // (2 * CR)
    chip_slots = 2 * CAP
    facet = lax.axis_index("facet")
    chips = lax.axis_size("facet") // 2
    chip = facet // 2
    core = facet % 2

    padded = -(-slots // 8) * 8
    number = lax.broadcasted_iota(jnp.int32, (padded, strip_rows), 0)
    message = number // chip_slots + 1
    owner = jnp.where(core == 0, chip, chip_to(message, chip, chips))
    slot = owner * chip_slots + number % chip_slots
    subgrids = slot_ref.shape[1]
    match = slot[:, :subgrids] == slot_ref[...]
    order = lax.broadcasted_iota(jnp.int32, match.shape, 1).astype(jnp.float32) + 1.0
    found = jnp.sum(jnp.where(match, order, 0.0), axis=1, keepdims=True)
    live = jnp.broadcast_to(jnp.where(found > 0.0, 1.0, 0.0), (padded, strip_rows))
    first = jnp.broadcast_to(jnp.maximum(found - 1.0, 0.0).astype(jnp.int32) * CR, (padded, strip_rows))

    step = 2.0 * math.pi / total

    def turn(product):
        if total & (total - 1) == 0:
            product = product & (total - 1)
        else:
            product = lax.rem(product, total)
        angle = step * product.astype(jnp.float32)
        return jnp.cos(angle), jnp.sin(angle)

    lane = lax.broadcasted_iota(jnp.int32, (padded, strip_rows), 1)
    row = lax.broadcasted_iota(jnp.int32, (CR, strip_rows), 0)
    for side in range(2):
        cell = (facet if side == 0 else facet ^ 1) * strip_rows + lane
        row_cos, row_sin = turn(row * cell[:1])
        first_cos, first_sin = turn(first * cell)
        first_cos, first_sin = first_cos * live, first_sin * live
        left = pl.ds(2 * side * strip_rows, strip_rows)
        right = pl.ds((2 * side + 1) * strip_rows, strip_rows)
        for c in range(slots):
            base_cos, base_sin = first_cos[c : c + 1], first_sin[c : c + 1]
            cos = (base_cos * row_cos - base_sin * row_sin).astype(jnp.bfloat16)
            sin = (base_sin * row_cos + base_cos * row_sin).astype(jnp.bfloat16)
            at = c * 2 * CR
            phase_ref[pl.ds(at, CR), left] = cos
            phase_ref[pl.ds(at, CR), right] = sin
            phase_ref[pl.ds(at + CR, CR), left] = -sin
            phase_ref[pl.ds(at + CR, CR), right] = cos

    partial_ref[...] = jnp.dot(
        phase_ref[:, : 2 * strip_rows], spec_ref[...], preferred_element_type=jnp.float32
    )


def term_kernel(core, first, scale, phase_ref, partial_ref, other_ref, *out_refs):
    depth = other_ref.shape[0]
    height = out_refs[0].shape[0]
    rows = slice(first * height, (first + len(out_refs)) * height)

    @pl.when(lax.axis_index("facet") % 2 == core)
    def _():
        terms = partial_ref[rows] + jnp.dot(
            phase_ref[rows, depth:], other_ref[...], preferred_element_type=jnp.float32
        )
        terms = (terms * scale).astype(jnp.bfloat16)
        for k, out_ref in enumerate(out_refs):
            out_ref[...] = terms[k * height : (k + 1) * height]


def weights_kernel(
    bands, slot_hbm, band_hbm, offset_hbm, weight_hbm, pos_hbm, after_ref, col_ref, row_ref, mix_ref,
    lane_ref, core_ref, slot_ref, band_ref, offset_ref, weight_ref, pos_ref, sems
):
    pairs = [
        (slot_hbm, slot_ref), (band_hbm, band_ref), (offset_hbm, offset_ref),
        (weight_hbm, weight_ref), (pos_hbm, pos_ref),
    ]
    copies = [pltpu.make_async_copy(a, b, sems.at[i]) for i, (a, b) in enumerate(pairs)]
    for copy in copies:
        copy.start()
    for copy in copies:
        copy.wait()
    blocks, width, points = col_ref.shape
    factor = -1.0 / (2.0 * kernel_sigma * kernel_sigma)
    tile = 512
    me = lax.axis_index("band")
    core_ref[...] = jnp.full(core_ref.shape, lax.axis_index("facet") % 2, jnp.int32)
    column = lax.broadcasted_iota(jnp.int32, (width, tile), 0).astype(jnp.float32)
    row = lax.broadcasted_iota(jnp.int32, (CR, tile), 0).astype(jnp.float32)
    for v in range(blocks):
        low = band_ref[v]
        slot = slot_ref[v]
        weight = weight_ref[v]
        for k in range(bands):
            band = band_from(k, me, bands)
            share = jnp.where(band == low, 1.0 - weight, jnp.where(band == low + 1, weight, 0.0))
            for c in range(CAP):
                mix_ref[v, k * CAP + c] = jnp.full((8, 128), jnp.where(slot == c, share, 0.0), jnp.float32)
        lane_ref[v] = offset_ref[v] + lax.broadcasted_iota(jnp.int32, (2 * CR, PC), 1)
        for t in range(0, points, tile):
            at = pl.ds(t, tile)
            diff = row - pos_ref[v, 0:1, at] * (CR - 1.0)
            row_ref[v, :, at] = jnp.exp(diff * diff * factor)
            diff = column - pos_ref[v, 1:2, at] * (PC - 1.0)
            col_ref[v, :, at] = jnp.exp(diff * diff * factor).astype(jnp.bfloat16)


def degrid_kernel(bands, mix_ref, lane_ref, col_ref, row_ref, sub_ref, swap_ref, *refs):
    band_refs, own_ref, out_ref = refs[: bands - 1], refs[bands - 1], refs[bands]
    height = 2 * CR
    share_rows = CAP * height
    core = lax.axis_index("facet") % 2
    parts = [jnp.where(core == 0, sub_ref[:share_rows], swap_ref[:share_rows])]
    own_ref[...] = parts[0]
    for k in range(1, bands):
        place = band_order(bands).index(k)
        at = pl.ds(place * share_rows, share_rows)
        parts.append(jnp.where(core == 0, swap_ref[at], band_refs[place][share_rows:]))
    held = [
        part[c * height : (c + 1) * height].astype(jnp.float32) for part in parts for c in range(CAP)
    ]
    for v in range(col_ref.shape[0]):
        halves = []
        for first in (0, HALF):
            mixed = None
            for i, sub in enumerate(held):
                share = jnp.concatenate([mix_ref[v, i]] * (height // 8), axis=0)
                part = sub[:, first : first + HALF] * share
                mixed = part if mixed is None else mixed + part
            halves.append(mixed)
        lane = lane_ref[v]
        within = lax.rem(lane, HALF)
        near, far = (jnp.take_along_axis(half, within, axis=1, mode="promise_in_bounds") for half in halves)
        patch = jnp.where(lane < HALF, near, far)
        partial = jnp.dot(
            patch.astype(jnp.bfloat16), col_ref[v], preferred_element_type=jnp.float32
        )
        out_ref[v, 0:1, :] = jnp.sum(partial[:CR] * row_ref[v], axis=0, keepdims=True)
        out_ref[v, 1:2, :] = jnp.sum(partial[CR:] * row_ref[v], axis=0, keepdims=True)


def local(
    facets, col_window, slot_of_subgrid, block_slot, block_band, block_offset, block_weight, vis_pos
):
    facet_count = lax.axis_size("facet")
    band_count = lax.axis_size("band")
    chips = facet_count // 2
    strip_rows = facets.shape[3]
    length = facets.shape[4]
    sky_rows = facet_count * strip_rows
    blocks, points = vis_pos.shape[2], vis_pos.shape[4]
    share_rows = CAP * 2 * CR
    height = 2 * share_rows
    chunks = 1
    core = lax.axis_index("facet") % 2

    def swap(x):
        return lax.ppermute(x, "facet", [(i, i ^ 1) for i in range(facet_count)])

    strip = facets.reshape(2 * strip_rows, length)
    seed = jnp.asarray(column_seed(length, SG))
    term_shape = jax.ShapeDtypeStruct((height, SG), jnp.bfloat16)
    spectrum = pl.pallas_call(
        functools.partial(front_kernel, chunks),
        out_shape=jax.ShapeDtypeStruct((2 * strip_rows, SG), jnp.bfloat16),
        in_specs=[HBM] * 3,
        out_specs=VMEM,
        scratch_shapes=[
            pltpu.VMEM((2 * strip_rows, length), jnp.bfloat16),
            pltpu.VMEM((length // 2, 2 * SG), jnp.bfloat16),
            pltpu.VMEM((1, length), jnp.float32),
            pltpu.VMEM(seed.shape, seed.dtype),
            pltpu.SemaphoreType.DMA((2 * chunks,)),
            pltpu.SemaphoreType.DMA((2,)),
        ],
        compiler_params=pltpu.CompilerParams(vmem_limit_bytes=32 * 2**20),
        name="front",
    )(*(
        pltpu.with_memory_space_constraint(x, pltpu.HBM)
        for x in (strip, col_window.reshape(1, length), seed)
    ))

    other = swap(spectrum)
    phase_rows = (chips - 1) * height
    phases, partial = pl.pallas_call(
        functools.partial(phase_kernel, sky_rows),
        out_shape=(
            jax.ShapeDtypeStruct((phase_rows, 4 * strip_rows), jnp.bfloat16),
            jax.ShapeDtypeStruct((phase_rows, SG), jnp.float32),
        ),
        in_specs=[VMEM] * 2,
        out_specs=(VMEM,) * 2,
        compiler_params=pltpu.CompilerParams(vmem_limit_bytes=32 * 2**20),
        name="phases",
    )(slot_of_subgrid.reshape(1, -1), spectrum)
    def make_terms(core, first, chip_count, name):
        return pl.pallas_call(
            functools.partial(term_kernel, core, first, 1.0 / math.sqrt(sky_rows)),
            out_shape=(term_shape,) * chip_count,
            in_specs=[VMEM] * 3,
            out_specs=(VMEM,) * chip_count,
            compiler_params=pltpu.CompilerParams(vmem_limit_bytes=16 * 2**20),
            name=name,
        )(phases, partial, other)

    terms = [make_terms(1, k - 1, 1, "terms")[0] for k in range(1, chips)]
    (own_terms,) = make_terms(0, 0, 1, "own_terms")
    arrived = [
        lax.ppermute(
            terms[k - 1],
            "facet",
            [
                (i, 2 * chip_to(k, i // 2, chips) if i % 2 else i + 1)
                for i in range(facet_count)
            ],
        )
        for k in range(1, chips)
    ]
    total = own_terms.astype(jnp.float32)
    for part in arrived[1:] + arrived[:1]:
        total = total + part.astype(jnp.float32)
    chip_subs = total.astype(jnp.bfloat16)

    col_kernel, row_kernel, mix, lanes, core_map = pl.pallas_call(
        functools.partial(weights_kernel, band_count),
        out_shape=(
            jax.ShapeDtypeStruct((blocks, PC, points), jnp.bfloat16),
            jax.ShapeDtypeStruct((blocks, CR, points), jnp.float32),
            jax.ShapeDtypeStruct((blocks, band_count * CAP, 8, 128), jnp.float32),
            jax.ShapeDtypeStruct((blocks, 2 * CR, PC), jnp.int32),
            jax.ShapeDtypeStruct((8, SG), jnp.int32),
        ),
        in_specs=[HBM] * 5 + [VMEM],
        out_specs=(VMEM,) * 5,
        scratch_shapes=[
            pltpu.SMEM((blocks,), jnp.int32),
            pltpu.SMEM((blocks,), jnp.int32),
            pltpu.SMEM((blocks,), jnp.int32),
            pltpu.SMEM((blocks,), jnp.float32),
            pltpu.VMEM((blocks, 2, points), jnp.float32),
            pltpu.SemaphoreType.DMA((5,)),
        ],
        compiler_params=pltpu.CompilerParams(vmem_limit_bytes=16 * 2**20),
        cost_estimate=pl.CostEstimate(
            flops=8 * blocks * PC * points, bytes_accessed=0, transcendentals=blocks * PC * points
        ),
        name="weights",
    )(
        *(
            pltpu.with_memory_space_constraint(x, pltpu.HBM)
            for x in (
                block_slot.reshape(blocks), block_band.reshape(blocks), block_offset.reshape(blocks),
                block_weight.reshape(blocks), vis_pos.reshape(blocks, 2, points),
            )
        ),
        chip_subs,
    )

    device = lambda band, facet: band * facet_count + facet
    band_subs = [
        lax.ppermute(
            chip_subs,
            ("band", "facet"),
            [
                (device(b, f), device(b, f - 1) if f % 2 else device(band_to(k, b, band_count), f + 1))
                for b in range(band_count)
                for f in range(facet_count)
            ],
        )
        for k in band_order(band_count)
    ]
    for_other = jnp.where(
        core_map[:1] == 0,
        jnp.concatenate([chip_subs[share_rows:]] * (band_count - 1)),
        jnp.concatenate([part[:share_rows] for part in band_subs]),
    )
    from_other = swap(for_other)
    owned, visible = pl.pallas_call(
        functools.partial(degrid_kernel, band_count),
        out_shape=(
            jax.ShapeDtypeStruct((share_rows, SG), jnp.bfloat16),
            jax.ShapeDtypeStruct((blocks, 2, points), jnp.float32),
        ),
        in_specs=[VMEM] * (5 + band_count),
        out_specs=(VMEM,) * 2,
        compiler_params=pltpu.CompilerParams(vmem_limit_bytes=24 * 2**20),
        name="degrid",
    )(mix, lanes, col_kernel, row_kernel, chip_subs, from_other, *band_subs)
    return (
        owned.reshape(1, CAP, 2, CR, SG),
        visible.reshape(1, 1, blocks, 2, points),
    )


def solution(mesh):
    in_specs = (
        P("band", "facet", None, None, None),
        P(),
        P(),
        P("band", "facet", None),
        P("band", "facet", None),
        P("band", "facet", None),
        P("band", "facet", None),
        P("band", "facet", None, None, None),
    )
    out_specs = (P("band", "facet", None, None, None), P("band", "facet", None, None, None))
    return jax.shard_map(local, mesh=mesh, in_specs=in_specs, out_specs=out_specs, check_vma=False)
```

```python
import functools
import math

import jax
import jax.numpy as jnp
import numpy as np
from jax import lax
from jax.experimental import pallas as pl
from jax.experimental.pallas import tpu as pltpu
from jax.sharding import PartitionSpec as P

SG = 256
CR = 16
CAP = 2
PC = 128
HALF = SG // 2

kernel_sigma = 1.5
VMEM = pl.BlockSpec(memory_space=pltpu.VMEM)
SMEM = pl.BlockSpec(memory_space=pltpu.SMEM)
HBM = pl.BlockSpec(memory_space=pltpu.HBM)


def chip_to(k, i, n):
    return i ^ k if n & (n - 1) == 0 else (i + k) % n


def band_to(k, i, n):
    return (i + k) % n


def band_from(k, i, n):
    return (i - k + n) % n


def column_seed(length, width):
    ratio = length // width
    place = (ratio * np.arange(width // 2)[None, :] - np.arange(ratio)[:, None])[:, :, None]
    out = []
    for parity in (0, 1):
        freq = np.arange(parity, width, 2)
        both = np.exp(2j * np.pi / length * (place * freq % length)).sum(-1)
        both = both / math.sqrt(length) / math.sqrt(width)
        out += [both.real, both.imag]
    return np.concatenate(out, axis=0).astype(jnp.bfloat16)


def front_kernel(
    chunks, facets_ref, window_hbm, seed_hbm, spec_ref,
    strip, table, window_ref, seed_ref, strip_sems, small_sems
):
    rows, length = strip.shape
    half = length // 2
    width = half // chunks
    strip_rows = rows // 2
    seed_copy = pltpu.make_async_copy(seed_hbm, seed_ref, small_sems.at[0])
    window_copy = pltpu.make_async_copy(window_hbm, window_ref, small_sems.at[1])
    seed_copy.start()
    copies = []
    for i in range(chunks):
        cols = pl.ds(i * width, width)
        upper = pl.ds(half + i * width, width)
        copies.append((
            pltpu.make_async_copy(facets_ref.at[:, cols], strip.at[:, cols], strip_sems.at[2 * i]),
            pltpu.make_async_copy(facets_ref.at[:, upper], strip.at[:, upper], strip_sems.at[2 * i + 1]),
        ))
    for group in copies:
        for copy in group:
            copy.start()
    window_copy.start()

    seed_copy.wait()
    ratio = length // SG
    lane = lax.broadcasted_iota(jnp.int32, (ratio, HALF), 1)
    for a in range(HALF):
        turned = pltpu.roll(seed_ref[...], a, 1) if a else seed_ref[...]
        at = pl.ds(a * ratio, ratio)
        for kind in range(4):
            part = turned[kind * ratio : (kind + 1) * ratio]
            if kind >= 2 and a:
                part = jnp.where(lane < a, -part, part)
            table[at, kind * HALF : (kind + 1) * HALF] = part.astype(jnp.bfloat16)

    window_copy.wait()
    even = odd = None
    for i in range(chunks):
        for copy in copies[i]:
            copy.wait()
        cols = pl.ds(i * width, width)
        upper = pl.ds(half + i * width, width)
        near = strip[:, cols].astype(jnp.float32) * window_ref[:, cols]
        far = strip[:, upper].astype(jnp.float32) * window_ref[:, upper]
        even_part = jnp.dot(
            (near + far).astype(jnp.bfloat16), table[cols, :SG], preferred_element_type=jnp.float32
        )
        odd_part = jnp.dot(
            (near - far).astype(jnp.bfloat16), table[cols, SG:], preferred_element_type=jnp.float32
        )
        even = even_part if even is None else even + even_part
        odd = odd_part if odd is None else odd + odd_part
    n = strip_rows
    even_real = even[:n, :HALF] - even[n:, HALF:]
    even_imag = even[:n, HALF:] + even[n:, :HALF]
    odd_real = odd[:n, :HALF] - odd[n:, HALF:]
    odd_imag = odd[:n, HALF:] + odd[n:, :HALF]
    spec_ref[:n, :HALF] = (even_real + odd_real).astype(jnp.bfloat16)
    spec_ref[:n, HALF:] = (even_real - odd_real).astype(jnp.bfloat16)
    spec_ref[n:, :HALF] = (even_imag + odd_imag).astype(jnp.bfloat16)
    spec_ref[n:, HALF:] = (even_imag - odd_imag).astype(jnp.bfloat16)


def phase_kernel(total, slot_ref, spec_ref, phase_ref, partial_ref):
    strip_rows = spec_ref.shape[0] // 2
    slots = phase_ref.shape[0] // (2 * CR)
    chip_slots = 2 * CAP
    facet = lax.axis_index("facet")
    chips = lax.axis_size("facet") // 2
    chip = facet // 2
    core = facet % 2

    padded = -(-slots // 8) * 8
    number = lax.broadcasted_iota(jnp.int32, (padded, strip_rows), 0)
    message = number // chip_slots + 1
    owner = jnp.where(core == 0, chip, chip_to(message, chip, chips))
    slot = owner * chip_slots + number % chip_slots
    subgrids = slot_ref.shape[1]
    match = slot[:, :subgrids] == slot_ref[...]
    order = lax.broadcasted_iota(jnp.int32, match.shape, 1).astype(jnp.float32) + 1.0
    found = jnp.sum(jnp.where(match, order, 0.0), axis=1, keepdims=True)
    live = jnp.broadcast_to(jnp.where(found > 0.0, 1.0, 0.0), (padded, strip_rows))
    first = jnp.broadcast_to(jnp.maximum(found - 1.0, 0.0).astype(jnp.int32) * CR, (padded, strip_rows))

    step = 2.0 * math.pi / total

    def turn(product):
        if total & (total - 1) == 0:
            product = product & (total - 1)
        else:
            product = lax.rem(product, total)
        angle = step * product.astype(jnp.float32)
        return jnp.cos(angle), jnp.sin(angle)

    lane = lax.broadcasted_iota(jnp.int32, (padded, strip_rows), 1)
    row = lax.broadcasted_iota(jnp.int32, (CR, strip_rows), 0)
    for side in range(2):
        cell = (facet if side == 0 else facet ^ 1) * strip_rows + lane
        row_cos, row_sin = turn(row * cell[:1])
        first_cos, first_sin = turn(first * cell)
        first_cos, first_sin = first_cos * live, first_sin * live
        left = pl.ds(2 * side * strip_rows, strip_rows)
        right = pl.ds((2 * side + 1) * strip_rows, strip_rows)
        for c in range(slots):
            base_cos, base_sin = first_cos[c : c + 1], first_sin[c : c + 1]
            cos = (base_cos * row_cos - base_sin * row_sin).astype(jnp.bfloat16)
            sin = (base_sin * row_cos + base_cos * row_sin).astype(jnp.bfloat16)
            at = c * 2 * CR
            phase_ref[pl.ds(at, CR), left] = cos
            phase_ref[pl.ds(at, CR), right] = sin
            phase_ref[pl.ds(at + CR, CR), left] = -sin
            phase_ref[pl.ds(at + CR, CR), right] = cos

    partial_ref[...] = jnp.dot(
        phase_ref[:, : 2 * strip_rows], spec_ref[...], preferred_element_type=jnp.float32
    )


def term_kernel(core, first, scale, phase_ref, partial_ref, other_ref, *out_refs):
    depth = other_ref.shape[0]
    height = out_refs[0].shape[0]
    rows = slice(first * height, (first + len(out_refs)) * height)

    @pl.when(lax.axis_index("facet") % 2 == core)
    def _():
        terms = partial_ref[rows] + jnp.dot(
            phase_ref[rows, depth:], other_ref[...], preferred_element_type=jnp.float32
        )
        terms = (terms * scale).astype(jnp.bfloat16)
        for k, out_ref in enumerate(out_refs):
            out_ref[...] = terms[k * height : (k + 1) * height]


def weights_kernel(
    bands, slot_hbm, band_hbm, offset_hbm, weight_hbm, pos_hbm, after_ref, col_ref, row_ref, mix_ref,
    lane_ref, core_ref, slot_ref, band_ref, offset_ref, weight_ref, pos_ref, sems
):
    pairs = [
        (slot_hbm, slot_ref), (band_hbm, band_ref), (offset_hbm, offset_ref),
        (weight_hbm, weight_ref), (pos_hbm, pos_ref),
    ]
    copies = [pltpu.make_async_copy(a, b, sems.at[i]) for i, (a, b) in enumerate(pairs)]
    for copy in copies:
        copy.start()
    for copy in copies:
        copy.wait()
    blocks, width, points = col_ref.shape
    factor = -1.0 / (2.0 * kernel_sigma * kernel_sigma)
    tile = 512
    me = lax.axis_index("band")
    core_ref[...] = jnp.full(core_ref.shape, lax.axis_index("facet") % 2, jnp.int32)
    column = lax.broadcasted_iota(jnp.int32, (width, tile), 0).astype(jnp.float32)
    row = lax.broadcasted_iota(jnp.int32, (CR, tile), 0).astype(jnp.float32)
    for v in range(blocks):
        low = band_ref[v]
        slot = slot_ref[v]
        weight = weight_ref[v]
        for k in range(bands):
            band = band_from(k, me, bands)
            share = jnp.where(band == low, 1.0 - weight, jnp.where(band == low + 1, weight, 0.0))
            for c in range(CAP):
                mix_ref[v, k * CAP + c] = jnp.full((8, 128), jnp.where(slot == c, share, 0.0), jnp.float32)
        lane_ref[v] = offset_ref[v] + lax.broadcasted_iota(jnp.int32, (2 * CR, PC), 1)
        for t in range(0, points, tile):
            at = pl.ds(t, tile)
            diff = row - pos_ref[v, 0:1, at] * (CR - 1.0)
            row_ref[v, :, at] = jnp.exp(diff * diff * factor)
            diff = column - pos_ref[v, 1:2, at] * (PC - 1.0)
            col_ref[v, :, at] = jnp.exp(diff * diff * factor).astype(jnp.bfloat16)


def degrid_kernel(bands, mix_ref, lane_ref, col_ref, row_ref, sub_ref, swap_ref, *refs):
    band_refs, own_ref, out_ref = refs[: bands - 1], refs[bands - 1], refs[bands]
    height = 2 * CR
    share_rows = CAP * height
    core = lax.axis_index("facet") % 2
    parts = [jnp.where(core == 0, sub_ref[:share_rows], swap_ref[:share_rows])]
    own_ref[...] = parts[0]
    for k in range(1, bands):
        at = pl.ds((bands - 1 - k) * share_rows, share_rows)
        parts.append(jnp.where(core == 0, swap_ref[at], band_refs[bands - 1 - k][share_rows:]))
    held = [
        part[c * height : (c + 1) * height].astype(jnp.float32) for part in parts for c in range(CAP)
    ]
    for v in range(col_ref.shape[0]):
        halves = []
        for first in (0, HALF):
            mixed = None
            for i, sub in enumerate(held):
                share = jnp.concatenate([mix_ref[v, i]] * (height // 8), axis=0)
                part = sub[:, first : first + HALF] * share
                mixed = part if mixed is None else mixed + part
            halves.append(mixed)
        lane = lane_ref[v]
        within = lax.rem(lane, HALF)
        near, far = (jnp.take_along_axis(half, within, axis=1, mode="promise_in_bounds") for half in halves)
        patch = jnp.where(lane < HALF, near, far)
        partial = jnp.dot(
            patch.astype(jnp.bfloat16), col_ref[v], preferred_element_type=jnp.float32
        )
        out_ref[v, 0:1, :] = jnp.sum(partial[:CR] * row_ref[v], axis=0, keepdims=True)
        out_ref[v, 1:2, :] = jnp.sum(partial[CR:] * row_ref[v], axis=0, keepdims=True)


def local(
    facets, col_window, slot_of_subgrid, block_slot, block_band, block_offset, block_weight, vis_pos
):
    facet_count = lax.axis_size("facet")
    band_count = lax.axis_size("band")
    chips = facet_count // 2
    strip_rows = facets.shape[3]
    length = facets.shape[4]
    sky_rows = facet_count * strip_rows
    blocks, points = vis_pos.shape[2], vis_pos.shape[4]
    share_rows = CAP * 2 * CR
    height = 2 * share_rows
    chunks = 1
    core = lax.axis_index("facet") % 2

    def swap(x):
        return lax.ppermute(x, "facet", [(i, i ^ 1) for i in range(facet_count)])

    strip = facets.reshape(2 * strip_rows, length)
    seed = jnp.asarray(column_seed(length, SG))
    term_shape = jax.ShapeDtypeStruct((height, SG), jnp.bfloat16)
    spectrum = pl.pallas_call(
        functools.partial(front_kernel, chunks),
        out_shape=jax.ShapeDtypeStruct((2 * strip_rows, SG), jnp.bfloat16),
        in_specs=[HBM] * 3,
        out_specs=VMEM,
        scratch_shapes=[
            pltpu.VMEM((2 * strip_rows, length), jnp.bfloat16),
            pltpu.VMEM((length // 2, 2 * SG), jnp.bfloat16),
            pltpu.VMEM((1, length), jnp.float32),
            pltpu.VMEM(seed.shape, seed.dtype),
            pltpu.SemaphoreType.DMA((2 * chunks,)),
            pltpu.SemaphoreType.DMA((2,)),
        ],
        compiler_params=pltpu.CompilerParams(vmem_limit_bytes=32 * 2**20),
        name="front",
    )(*(
        pltpu.with_memory_space_constraint(x, pltpu.HBM)
        for x in (strip, col_window.reshape(1, length), seed)
    ))

    other = swap(spectrum)
    phase_rows = (chips - 1) * height
    phases, partial = pl.pallas_call(
        functools.partial(phase_kernel, sky_rows),
        out_shape=(
            jax.ShapeDtypeStruct((phase_rows, 4 * strip_rows), jnp.bfloat16),
            jax.ShapeDtypeStruct((phase_rows, SG), jnp.float32),
        ),
        in_specs=[VMEM] * 2,
        out_specs=(VMEM,) * 2,
        compiler_params=pltpu.CompilerParams(vmem_limit_bytes=32 * 2**20),
        name="phases",
    )(slot_of_subgrid.reshape(1, -1), spectrum)
    def make_terms(core, first, chip_count, name):
        return pl.pallas_call(
            functools.partial(term_kernel, core, first, 1.0 / math.sqrt(sky_rows)),
            out_shape=(term_shape,) * chip_count,
            in_specs=[VMEM] * 3,
            out_specs=(VMEM,) * chip_count,
            compiler_params=pltpu.CompilerParams(vmem_limit_bytes=16 * 2**20),
            name=name,
        )(phases, partial, other)

    terms = [make_terms(1, k - 1, 1, "terms")[0] for k in range(1, chips)]
    (own_terms,) = make_terms(0, 0, 1, "own_terms")
    arrived = [
        lax.ppermute(
            terms[k - 1],
            "facet",
            [
                (i, 2 * chip_to(k, i // 2, chips) if i % 2 else i + 1)
                for i in range(facet_count)
            ],
        )
        for k in range(1, chips)
    ]
    total = own_terms.astype(jnp.float32)
    for part in arrived[1:] + arrived[:1]:
        total = total + part.astype(jnp.float32)
    chip_subs = total.astype(jnp.bfloat16)

    col_kernel, row_kernel, mix, lanes, core_map = pl.pallas_call(
        functools.partial(weights_kernel, band_count),
        out_shape=(
            jax.ShapeDtypeStruct((blocks, PC, points), jnp.bfloat16),
            jax.ShapeDtypeStruct((blocks, CR, points), jnp.float32),
            jax.ShapeDtypeStruct((blocks, band_count * CAP, 8, 128), jnp.float32),
            jax.ShapeDtypeStruct((blocks, 2 * CR, PC), jnp.int32),
            jax.ShapeDtypeStruct((8, SG), jnp.int32),
        ),
        in_specs=[HBM] * 5 + [VMEM],
        out_specs=(VMEM,) * 5,
        scratch_shapes=[
            pltpu.SMEM((blocks,), jnp.int32),
            pltpu.SMEM((blocks,), jnp.int32),
            pltpu.SMEM((blocks,), jnp.int32),
            pltpu.SMEM((blocks,), jnp.float32),
            pltpu.VMEM((blocks, 2, points), jnp.float32),
            pltpu.SemaphoreType.DMA((5,)),
        ],
        compiler_params=pltpu.CompilerParams(vmem_limit_bytes=16 * 2**20),
        cost_estimate=pl.CostEstimate(
            flops=8 * blocks * PC * points, bytes_accessed=0, transcendentals=blocks * PC * points
        ),
        name="weights",
    )(
        *(
            pltpu.with_memory_space_constraint(x, pltpu.HBM)
            for x in (
                block_slot.reshape(blocks), block_band.reshape(blocks), block_offset.reshape(blocks),
                block_weight.reshape(blocks), vis_pos.reshape(blocks, 2, points),
            )
        ),
        chip_subs,
    )

    device = lambda band, facet: band * facet_count + facet
    band_subs = [
        lax.ppermute(
            chip_subs,
            ("band", "facet"),
            [
                (device(b, f), device(b, f - 1) if f % 2 else device(band_to(k, b, band_count), f + 1))
                for b in range(band_count)
                for f in range(facet_count)
            ],
        )
        for k in range(1, band_count)
    ][::-1]
    for_other = jnp.where(
        core_map[:1] == 0,
        jnp.concatenate([chip_subs[share_rows:]] * (band_count - 1)),
        jnp.concatenate([part[:share_rows] for part in band_subs]),
    )
    from_other = swap(for_other)
    owned, visible = pl.pallas_call(
        functools.partial(degrid_kernel, band_count),
        out_shape=(
            jax.ShapeDtypeStruct((share_rows, SG), jnp.bfloat16),
            jax.ShapeDtypeStruct((blocks, 2, points), jnp.float32),
        ),
        in_specs=[VMEM] * (5 + band_count),
        out_specs=(VMEM,) * 2,
        compiler_params=pltpu.CompilerParams(vmem_limit_bytes=24 * 2**20),
        name="degrid",
    )(mix, lanes, col_kernel, row_kernel, chip_subs, from_other, *band_subs)
    return (
        owned.reshape(1, CAP, 2, CR, SG),
        visible.reshape(1, 1, blocks, 2, points),
    )


def solution(mesh):
    in_specs = (
        P("band", "facet", None, None, None),
        P(),
        P(),
        P("band", "facet", None),
        P("band", "facet", None),
        P("band", "facet", None),
        P("band", "facet", None),
        P("band", "facet", None, None, None),
    )
    out_specs = (P("band", "facet", None, None, None), P("band", "facet", None, None, None))
    return jax.shard_map(local, mesh=mesh, in_specs=in_specs, out_specs=out_specs, check_vma=False)
```
